256 devices in a mesh: dp: 2 (over core), head: 8 (over x, z_lo), ctx: 16 (over y, z_hi).
Axes of the slice: x: 4, y: 4, z: 8 (z_hi: 4, z_lo: 2; z = z_hi * 2 + z_lo), core: 2. Of those that a mesh axis runs over, the one named last changes fastest.
Arguments:
- query_states: bfloat16 [2, 16384, 32, 128], P('dp', 'ctx', 'head'), may hold values from -6 to 6
- key_states: bfloat16 [2, 16384, 8, 128], P('dp', 'ctx', 'head'), may hold values from -6 to 6
- value_states: bfloat16 [2, 16384, 8, 128], P('dp', 'ctx', 'head'), may hold values from -12 to 12
- gate_values: float32 [32], P('head'), may hold values from 0.1 to 0.9
- head_flags: int32 [32], P('head'), may hold values from 0 to 1, as said below
- output_grad: bfloat16 [2, 16384, 32, 128], P('dp', 'ctx', 'head'), may hold values from -16 to 16
Outputs:
- blended: bfloat16 [2, 16384, 32, 128], P('dp', 'ctx', 'head')
- gate_grad: float32 [32], replicated
The draws below stay inside these ranges and needn't reach their ends.
Inputs may be any that keep to these rules, and one draw needn't show every extreme that they name: `head_flags`: exactly 1 of the 4 query heads of each key-value head have flag 1.
All inputs are finite; a program needn't handle non-finite values.
Results may differ from the reference program's by a relative error of at most 0.005.
Values may be sent and summed in bfloat16 or wider, within the bound.
No kernel may reach another device: no remote copies, remote signals or barrier semaphores. Data moves between devices by JAX's collectives and lax.ppermute only.
A program may use at most 64 MiB of HBM per device.

```python
import math
import jax
import jax.numpy as jnp
from jax import lax

HD = 128
KVH = 8
QPG = 4
RET = 1
SINK = 64
WINDOW = 2048
SEQS = 2
L = 16384
H = 32


def draw_query_states(seed_key, part_index):
    own_key = jax.random.fold_in(seed_key, 11)
    drawn = 1.5 * jax.random.normal(jax.random.fold_in(own_key, 3), (SEQS, L, H, HD), jnp.float32)
    return jnp.clip(drawn, -6.0, 6.0).astype(jnp.bfloat16)


def draw_key_states(seed_key, part_index):
    own_key = jax.random.fold_in(seed_key, 21)
    sink_scale = jnp.where(jnp.arange(L) < SINK, 1.8, 1.0).astype(jnp.float32)[None, :, None, None]
    drawn = jax.random.normal(jax.random.fold_in(own_key, 2), (SEQS, L, KVH, HD), jnp.float32) * sink_scale
    return jnp.clip(drawn, -6.0, 6.0).astype(jnp.bfloat16)


def draw_output_grad(seed_key, part_index):
    own_key = jax.random.fold_in(seed_key, 31)
    fraction = (jnp.arange(L, dtype=jnp.float32) / (L - 1))[None, :, None, None]
    ramp_scale = jnp.exp(fraction * math.log(3.0))
    drawn = jnp.clip(jax.random.normal(jax.random.fold_in(own_key, 3), (SEQS, L, H, HD), jnp.float32), -5.0, 5.0) * ramp_scale
    return drawn.astype(jnp.bfloat16)


def pick_order(split_key):
    return jax.random.permutation(split_key, QPG)


def draw_head_flags(seed_key, part_index):
    split_keys = jax.random.split(jax.random.fold_in(seed_key, 41), KVH)
    orders = jax.vmap(pick_order)(split_keys)
    return (orders < RET).astype(jnp.int32).reshape(H)


def shard_levels(rng, shape, cuts, least, top_value):
    def one(dim, blocks):
        heights = jax.random.uniform(jax.random.fold_in(jax.random.fold_in(rng, 6), dim), (blocks,), jnp.float32, least / len(cuts), top_value / len(cuts))
        return jnp.repeat(jnp.exp(heights), shape[dim] // blocks).reshape((-1,) + (1,) * (len(shape) - dim - 1))

    gain = one(*cuts[0])
    for cut in cuts[1:]:
        gain = gain * one(*cut)
    return gain


def gaussian(key, dims, scale, limit, cuts=(), held_as=jnp.bfloat16):
    values = scale * jax.random.normal(key, dims, jnp.float32)
    if cuts:
        values = values * shard_levels(key, dims, cuts, -0.22, 0.18)
    return jnp.clip(values, -limit, limit).astype(held_as)


def setup_inputs(seed: int = 0) -> dict:
    key_of = jax.random.split(jax.random.key(seed), 7)
    return {
        "query_states": draw_query_states(jax.random.fold_in(key_of[6], 71), 0),
        "key_states": draw_key_states(jax.random.fold_in(key_of[6], 71), 0),
        "value_states": gaussian(key_of[2], (SEQS, L, KVH, HD), 2.0, 12.0, ((0, 2), (1, 16), (2, 8))),
        "gate_values": jnp.clip(0.1 + 0.79999997 * jax.random.uniform(key_of[3], (H,), jnp.float32) ** shard_levels(key_of[3], (H,), ((0, 8),), -0.2, 0.2), 0.1, 0.9),
        "head_flags": draw_head_flags(jax.random.fold_in(key_of[6], 71), 0),
        "output_grad": draw_output_grad(jax.random.fold_in(key_of[6], 71), 0),
    }


def weighted_mix(query_block, key_rows, value_rows, allowed):
    scores = jnp.einsum('rgeh,kgh->rgek', query_block.astype(jnp.float32), key_rows.astype(jnp.float32)) * (1.0 / math.sqrt(HD))
    visible = allowed[:, None, None, :]
    scores = jnp.where(visible, scores, -jnp.inf)
    highest = lax.optimization_barrier(jnp.max(scores, axis=-1, keepdims=True))
    weights = jnp.where(visible, jnp.exp(scores - highest), 0.0)
    denominator = lax.optimization_barrier(jnp.sum(weights, axis=-1))
    rounded = lax.optimization_barrier(weights.astype(jnp.bfloat16)).astype(jnp.float32)
    numerator = jnp.einsum('rgek,kgh->rgeh', rounded, value_rows.astype(jnp.float32))
    return numerator / denominator[..., None]

def one_sequence(picker, query_seq, key_seq, value_seq):
    row_block = math.gcd(L, 512)
    positions = jnp.arange(L, dtype=jnp.int32)
    chosen = jnp.einsum('gre,lgeh->lgrh', picker, query_seq.astype(jnp.float32), precision=lax.Precision.HIGHEST)
    starts = jnp.arange(L // row_block, dtype=jnp.int32) * row_block

    def full_block(first_row):
        row_pos = first_row + jnp.arange(row_block, dtype=jnp.int32)
        query_block = lax.dynamic_slice_in_dim(chosen, first_row, row_block)
        return weighted_mix(query_block, key_seq, value_seq, positions[None, :] <= row_pos[:, None])
    full_ret = lax.map(full_block, starts).reshape(L, KVH, RET, HD)
    full_all = jnp.einsum('gre,lgrh->lgeh', picker, full_ret, precision=lax.Precision.HIGHEST)
    pad_keys = jnp.concatenate([jnp.zeros((WINDOW, KVH, HD), key_seq.dtype), key_seq], axis=0)
    pad_values = jnp.concatenate([jnp.zeros((WINDOW, KVH, HD), value_seq.dtype), value_seq], axis=0)
    sink_pos = jnp.arange(SINK, dtype=jnp.int32)

    def near_block(first_row):
        row_pos = first_row + jnp.arange(row_block, dtype=jnp.int32)
        query_block = lax.dynamic_slice_in_dim(query_seq, first_row, row_block)
        near_pos = first_row - WINDOW + jnp.arange(WINDOW + row_block, dtype=jnp.int32)
        near_ok = (near_pos[None, :] >= 0) & (near_pos[None, :] <= row_pos[:, None]) & (row_pos[:, None] - near_pos[None, :] < WINDOW)
        sink_ok = (sink_pos[None, :] <= row_pos[:, None]) & (row_pos[:, None] - sink_pos[None, :] >= WINDOW)
        key_rows = jnp.concatenate([key_seq[:SINK], lax.dynamic_slice_in_dim(pad_keys, first_row, WINDOW + row_block)], axis=0)
        value_rows = jnp.concatenate([value_seq[:SINK], lax.dynamic_slice_in_dim(pad_values, first_row, WINDOW + row_block)], axis=0)
        return weighted_mix(query_block, key_rows, value_rows, jnp.concatenate([sink_ok, near_ok], axis=1))
    near_all = lax.map(near_block, starts).reshape(L, KVH, QPG, HD)
    return (full_all, near_all)

def reference(query_states, key_states, value_states, gate_values, head_flags, output_grad):
    marked = head_flags.reshape(KVH, QPG)
    ordinal = jnp.cumsum(marked, axis=1) - 1
    slot_ids = jnp.arange(RET, dtype=jnp.int32)
    picker = ((marked[:, None, :] == 1) & (ordinal[:, None, :] == slot_ids[None, :, None])).astype(jnp.float32)
    queries = query_states.reshape(SEQS, L, KVH, QPG, HD)

    def per_sequence(members):
        return one_sequence(picker, members[0], members[1], members[2])
    full_all, near_all = lax.map(per_sequence, (queries, key_states, value_states))
    gate_cols = gate_values.reshape(KVH, QPG)[:, :, None]
    retrieval = (marked == 1)[:, :, None]
    mixed = jnp.where(retrieval, gate_cols * full_all + (1.0 - gate_cols) * near_all, near_all)
    blended = mixed.astype(jnp.bfloat16).reshape(SEQS, L, H, HD)
    grad_rows = output_grad.reshape(SEQS, L, KVH, QPG, HD).astype(jnp.float32)
    gate_terms = lax.optimization_barrier(jnp.sum(grad_rows * (full_all - near_all), axis=(0, 1, 4))) * marked.astype(jnp.float32)
    gate_grad = gate_terms.reshape(H) * (1.0 / math.sqrt(SEQS * L * HD))
    return (blended, gate_grad)
```

```python
import functools
import math

import jax
import jax.numpy as jnp
from jax import lax
from jax.experimental import pallas as pl
from jax.experimental.pallas import tpu as pltpu
from jax.sharding import PartitionSpec as P

SINK = 64
WINDOW = 2048
BLOCK = 1024
TILE = 512
DEPTH = 3
LANES = 128
TAIL = 32
VMEM = pltpu.VMEM
LOG2E = 1.4426950408889634
NEG = -1e30


def params():
    return pltpu.CompilerParams(vmem_limit_bytes=48 * 2**20)


def cost(units, bytes_accessed=4 * 2**20):
    return pl.CostEstimate(
        flops=int(units * 4 * BLOCK * BLOCK * LANES),
        bytes_accessed=bytes_accessed,
        transcendentals=int(units * BLOCK * BLOCK),
    )


def scores_of(q, k):
    return lax.dot_general(q, k, (((1,), (1,)), ((), ())), preferred_element_type=jnp.float32)


def fold(carried, scores, values, scale):
    top, total, acc = carried
    newest = jnp.maximum(top, jnp.max(scores, axis=1, keepdims=True) * scale)
    weights = jnp.exp2(scores * scale - newest)
    factor = jnp.exp2(top - newest)
    total = total * factor + jnp.sum(weights, axis=1, keepdims=True)
    acc = acc * factor + jnp.dot(
        weights.astype(jnp.bfloat16), values, preferred_element_type=jnp.float32
    )
    return newest, total, acc


def early_kernel(scale, at, q0, q1, q2, q3, k0, k1, k3, v0, v1, v3, acc_ref, ml_ref, qs, ks, vs):
    index = at[0]
    sets = 4 - index // 4
    for n, ref in enumerate((q0, q1, q2, q3)):
        qs[pl.ds(n * BLOCK, BLOCK), :] = ref[...]
    for n, (kref, vref) in enumerate(((k1, v1), (k3, v3))):
        ks[pl.ds(n * BLOCK, BLOCK), :] = kref[...]
        vs[pl.ds(n * BLOCK, BLOCK), :] = vref[...]
    more = jnp.where(index >= 3, 2, jnp.where(index >= 1, 1, 0))
    row = lax.broadcasted_iota(jnp.int32, (TILE, BLOCK), 0)
    col = lax.broadcasted_iota(jnp.int32, (TILE, BLOCK), 1)
    ahead = col - row

    def tile(t, _):
        rows = pl.ds(pl.multiple_of(t * TILE, TILE), TILE)
        q = qs[rows, :]
        limit = jnp.where(t < BLOCK // TILE, t * TILE, BLOCK)
        scores = jnp.where(ahead <= limit, scores_of(q, k0[...]), NEG)
        start = (
            jnp.full((TILE, 1), NEG, jnp.float32),
            jnp.zeros((TILE, 1), jnp.float32),
            jnp.zeros((TILE, LANES), jnp.float32),
        )
        state = fold(start, scores, v0[...], scale)

        def block(b, carried):
            keys = pl.ds(pl.multiple_of(b * BLOCK, BLOCK), BLOCK)
            return fold(carried, scores_of(q, ks[keys, :]), vs[keys, :], scale)

        top, total, acc = lax.fori_loop(0, more, block, state)
        acc_ref[rows, :] = acc
        lane = lax.broadcasted_iota(jnp.int32, (TILE, LANES), 1)
        ml_ref[rows, :] = jnp.where(lane < LANES // 2, top, total)
        return 0

    lax.fori_loop(0, sets * (BLOCK // TILE), tile, 0)


def late_kernel(scale, at, q0, q1, q2, q3, k2, v2, acc_ref, ml_ref, own_ref, lse_ref, p1, p2, p3, qs, ps, ls):
    index = at[0]
    sets = 4 - index // 4
    for n, ref in enumerate((q0, q1, q2, q3)):
        qs[pl.ds(n * BLOCK, BLOCK), :] = ref[...]

    def tile(t, _):
        rows = pl.ds(pl.multiple_of(t * TILE, TILE), TILE)
        q = qs[rows, :]
        ml = ml_ref[rows, :]
        state = (ml[:, 0:1], ml[:, LANES // 2 : LANES // 2 + 1], acc_ref[rows, :])

        def block(b, carried):
            return fold(carried, scores_of(q, k2[...]), v2[...], scale)

        top, total, acc = lax.fori_loop(0, jnp.where(index >= 2, 1, 0), block, state)
        out = acc / total
        lse = jnp.broadcast_to(top + jnp.log2(total), (TILE, LANES))

        @pl.when(t < BLOCK // TILE)
        def _():
            own_ref[rows, :] = out
            lse_ref[rows, :] = lse

        ps[rows, :] = out.astype(jnp.bfloat16)
        for g in range(TILE // LANES):
            turned = lse[g * LANES : (g + 1) * LANES, :].T
            ls[pl.ds(t * (TILE // LANES) + g, 1), :] = turned[0:1, :]
        return 0

    lax.fori_loop(0, sets * (BLOCK // TILE), tile, 0)
    for n, ref in ((1, p1), (2, p2), (3, p3)):

        @pl.when(n < sets)
        def _():
            ref[0:BLOCK, :] = ps[n * BLOCK : (n + 1) * BLOCK, :]
            value = ls[n * 8 : (n + 1) * 8, :]
            high = value.astype(jnp.bfloat16).astype(jnp.float32)
            rest = value - high
            middle = rest.astype(jnp.bfloat16).astype(jnp.float32)
            ref[BLOCK : BLOCK + TAIL, :] = jnp.concatenate(
                [high, middle, rest - middle, jnp.zeros_like(high)], axis=0
            ).astype(jnp.bfloat16)

        @pl.when(n >= sets)
        def _():
            ref[...] = jnp.zeros_like(ref)


def near_kernel(scale, per_pos, positions, out_dtype, at, q, k0, k1, k2, v0, v1, v2, sinks, out_ref, ks, vs):
    index = at[0]
    for n, (kref, vref) in enumerate(((k2, v2), (k1, v1), (k0, v0))):
        ks[pl.ds(n * BLOCK, BLOCK), :] = kref[...]
        vs[pl.ds(n * BLOCK, BLOCK), :] = vref[...]
    tile = positions * per_pos
    width = WINDOW + positions
    row = lax.broadcasted_iota(jnp.int32, (tile, positions), 0) // per_pos
    col = lax.broadcasted_iota(jnp.int32, (tile, positions), 1)
    sink_row = lax.broadcasted_iota(jnp.int32, (tile, LANES), 0) // per_pos
    sink_col = lax.broadcasted_iota(jnp.int32, (tile, LANES), 1)
    sink_k = sinks[0:LANES, :]
    sink_v = sinks[LANES : 2 * LANES, :]
    first = (2 - index) * BLOCK

    def visit(t, _):
        rows = pl.ds(pl.multiple_of(t * tile, tile), tile)
        begin = pl.multiple_of(t * positions, positions)
        keys = pl.ds(begin, width)
        query = q[rows, :]
        s = scores_of(query, ks[keys, :])
        column = lax.broadcasted_iota(jnp.int32, (1, width), 1) + begin
        s = s + jnp.where(column >= first, 0.0, NEG)
        head = jnp.where(col > row, s[:, :positions], NEG)
        mid = s[:, positions:WINDOW]
        last = jnp.where(col <= row, s[:, WINDOW:], NEG)
        far = scores_of(query, sink_k)
        reach = index * BLOCK + begin + sink_row - sink_col
        far = jnp.where((sink_col < SINK) & (reach >= WINDOW), far, NEG)
        s = jnp.concatenate([head, mid, last, far], axis=1)
        top = jnp.max(s, axis=1, keepdims=True) * scale
        w = jnp.exp2(s * scale - top)
        total = jnp.sum(w, axis=1, keepdims=True)
        w = w.astype(jnp.bfloat16)
        acc = jnp.dot(w[:, :width], vs[keys, :], preferred_element_type=jnp.float32)
        acc = acc + jnp.dot(w[:, width:], sink_v, preferred_element_type=jnp.float32)
        out_ref[rows, :] = (acc / total).astype(out_dtype)
        return 0

    lax.fori_loop(0, BLOCK // positions, visit, 0)


def merge_kernel(norm, at, gate, own, lse, p1, p2, p3, near, grad, mix_ref, row_ref):
    index = at[0]
    spot = at[1]
    level = index // 4
    gated = gate[0]
    terms = []
    for n, ref in ((1, p1), (2, p2), (3, p3)):
        tail = ref[BLOCK : BLOCK + TAIL, :].astype(jnp.float32)
        value = tail[0:8] + tail[8:16] + tail[16:24]
        terms.append(jnp.where(level >= n, value, NEG))
    total = jnp.zeros((1, LANES), jnp.float32)
    for g in range(BLOCK // LANES):
        rows = slice(g * LANES, (g + 1) * LANES)
        logs = [lse[rows, :]]
        for value in terms:
            logs.append(jnp.broadcast_to(value[g : g + 1, :], (LANES, LANES)).T)
        top = functools.reduce(jnp.maximum, logs)
        shares = [jnp.exp2(x - top) for x in logs]
        acc = shares[0] * own[rows, :]
        for share, ref in zip(shares[1:], (p1, p2, p3)):
            acc = acc + share * ref[rows, :].astype(jnp.float32)
        full = acc / functools.reduce(jnp.add, shares)
        close = near[rows, :]
        mix_ref[rows, :] = (gated * full + (1.0 - gated) * close).astype(jnp.bfloat16)
        total = total + jnp.sum(
            grad[rows, :].astype(jnp.float32) * (full - close), axis=0, keepdims=True
        )
    value = jnp.sum(total, axis=1, keepdims=True) * norm
    lane = lax.broadcasted_iota(jnp.int32, row_ref.shape, 1)
    row_ref[...] = jnp.where(lane == spot, value, 0.0)


def call(kernel, scalars, arrays, outs, scratch, estimate):
    specs = [pl.BlockSpec(memory_space=pltpu.SMEM)] * len(scalars)
    specs += [pl.BlockSpec(memory_space=VMEM)] * len(arrays)
    return pl.pallas_call(
        kernel,
        out_shape=outs,
        in_specs=specs,
        out_specs=[pl.BlockSpec(memory_space=VMEM)] * len(outs),
        scratch_shapes=scratch,
        compiler_params=params(),
        cost_estimate=estimate,
    )(*scalars, *arrays)


def shape(rows, dtype):
    return jax.ShapeDtypeStruct((rows, LANES), dtype)


def on_device(query_states, key_states, value_states, gate_values, head_flags, output_grad):
    bf16, f32 = jnp.bfloat16, jnp.float32
    heads = head_flags.shape[0]
    ctx = lax.axis_size("ctx")
    index = lax.axis_index("ctx")
    scale = LOG2E / math.sqrt(LANES)
    keys = key_states.reshape(BLOCK, LANES)
    values = value_states.reshape(BLOCK, LANES)
    marked = (head_flags == 1)[None, :, None]
    which = jnp.sum(head_flags * jnp.arange(heads, dtype=jnp.int32))

    def pick(array):
        return jnp.sum(jnp.where(marked, array[0].astype(f32), 0.0), axis=1).astype(bf16)

    def ring(block, shift):
        return lax.ppermute(block, "ctx", [(i, (i + shift) % ctx) for i in range(ctx)])

    k1, v3 = ring(keys, 1), ring(values, 3)
    v1, k3 = ring(values, 1), ring(keys, 3)
    query = pick(query_states)
    visitors = [
        lax.ppermute(query, "ctx", [(i, i - 4 * n) for i in range(4 * n, ctx)])
        for n in range(1, DEPTH + 1)
    ]
    k2, v2 = ring(k1, 1), ring(v3, -1)
    pad = jnp.zeros((LANES - SINK, LANES), bf16)
    sinks = jnp.concatenate([keys[:SINK], pad, values[:SINK], pad], axis=0)
    reach = ctx
    while reach > 1:
        half = reach // 2
        got = lax.ppermute(sinks, "ctx", [(i, i + half) for i in range(0, ctx, reach)])
        sinks = jnp.where(index % reach == half, got, sinks)
        reach = half
    grad = pick(output_grad)
    at = jnp.stack([index, lax.axis_index("head") * heads + which]).astype(jnp.int32)
    gate = jnp.sum(jnp.where(head_flags == 1, gate_values, 0.0))[None]

    full_rows = (DEPTH + 1) * BLOCK
    acc, ml = call(
        functools.partial(early_kernel, scale),
        [at],
        [query, *visitors, keys, k1, k3, values, v1, v3],
        [shape(full_rows, f32), shape(full_rows, f32)],
        [VMEM((full_rows, LANES), bf16), VMEM((2 * BLOCK, LANES), bf16), VMEM((2 * BLOCK, LANES), bf16)],
        cost(12),
    )
    own, lse, *parts = call(
        functools.partial(late_kernel, scale),
        [at],
        [query, *visitors, k2, v2, acc, ml],
        [shape(BLOCK, f32), shape(BLOCK, f32)] + [shape(BLOCK + TAIL, bf16)] * DEPTH,
        [VMEM((full_rows, LANES), bf16), VMEM((full_rows, LANES), bf16), VMEM((8 * (DEPTH + 1), LANES), f32)],
        cost(4),
    )
    returned = [
        lax.ppermute(part, "ctx", [(i - 4 * n, i) for i in range(4 * n, ctx)])
        for n, part in enumerate(parts, 1)
    ]
    window = [keys, k1, k2, values, v1, v2, sinks]
    scratch = [VMEM((3 * BLOCK, LANES), bf16), VMEM((3 * BLOCK, LANES), bf16)]
    [near_one] = call(
        functools.partial(near_kernel, scale, 1, 256, f32),
        [at],
        [query, *window],
        [shape(BLOCK, f32)],
        scratch,
        cost(2.3),
    )
    [near_all] = call(
        functools.partial(near_kernel, scale, heads, 128, bf16),
        [at],
        [query_states.reshape(BLOCK * heads, LANES), *window],
        [shape(BLOCK * heads, bf16)],
        scratch,
        cost(9),
    )
    norm = 1.0 / math.sqrt(lax.axis_size("dp") * BLOCK * ctx * LANES)
    devices = lax.axis_size("dp") * lax.axis_size("head") * ctx
    mixed, row = call(
        functools.partial(merge_kernel, norm),
        [at, gate],
        [own, lse, *returned, near_one, grad],
        [shape(BLOCK, bf16), shape(devices, f32)],
        [],
        cost(0.1),
    )
    everyone = lax.all_to_all(row, ("dp", "head", "ctx"), 0, 0, tiled=True)
    gate_grad = jnp.sum(everyone, axis=0)[: heads * lax.axis_size("head")]
    near_all = near_all.reshape(1, BLOCK, heads, LANES)
    blended = jnp.where(marked[None], mixed[None, :, None, :], near_all)
    return (blended, gate_grad)


def solution(mesh):
    spec = P("dp", "ctx", "head", None)
    return jax.shard_map(
        on_device,
        mesh=mesh,
        in_specs=(spec, spec, spec, P("head"), P("head"), spec),
        out_specs=(spec, P()),
        check_vma=False,
    )
```

```python
import functools
import math

import jax
import jax.numpy as jnp
from jax import lax
from jax.experimental import pallas as pl
from jax.experimental.pallas import tpu as pltpu
from jax.sharding import PartitionSpec as P

SINK = 64
WINDOW = 2048
BLOCK = 1024
TILE = 512
UNROLL = 2
CHUNK = 512
ROWS = 8
DEPTH = 3
LANES = 128
VMEM = pltpu.VMEM
LOG2E = 1.4426950408889634
NEG = -1e30


def params():
    return pltpu.CompilerParams(vmem_limit_bytes=32 * 2**20)


def cost(units, bytes_accessed=4 * 2**20):
    return pl.CostEstimate(
        flops=int(units * 4 * BLOCK * BLOCK * LANES),
        bytes_accessed=bytes_accessed,
        transcendentals=int(units * BLOCK * BLOCK),
    )


def scores_of(q, k):
    return lax.dot_general(q, k, (((1,), (1,)), ((), ())), preferred_element_type=jnp.float32)


def fold(carried, scores, values, scale):
    top, total, acc = carried
    newest = jnp.maximum(top, jnp.max(scores, axis=1, keepdims=True) * scale)
    weights = jnp.exp2(scores * scale - newest).astype(jnp.bfloat16)
    factor = jnp.exp2(top - newest)
    update = jnp.dot(weights, values, preferred_element_type=jnp.float32)
    return newest, total * factor + update[:, LANES:], acc * factor + update[:, :LANES]


def one_pass(scores, values, scale, before=None):
    top = functools.reduce(
        jnp.maximum, [jnp.max(s, axis=1, keepdims=True) for s in scores]
    ) * scale
    if before is not None:
        top = jnp.maximum(top, before[0])
    update = functools.reduce(
        jnp.add,
        [
            jnp.dot(
                jnp.exp2(s * scale - top).astype(jnp.bfloat16),
                v,
                preferred_element_type=jnp.float32,
            )
            for s, v in zip(scores, values)
        ],
    )
    total, acc = update[:, LANES:], update[:, :LANES]
    if before is not None:
        factor = jnp.exp2(before[0] - top)
        total = total + before[1] * factor
        acc = acc + before[2] * factor
    return top, total, acc


def put_values(dest, first, source):
    rows = source.shape[0]
    dest[pl.ds(first, rows), 0:LANES] = source
    dest[pl.ds(first, rows), LANES : 2 * LANES] = jnp.ones((rows, LANES), jnp.bfloat16)


def early_kernel(scale, at, q0, q1, q2, q3, kv0, kv1, kv3, acc_ref, ml_ref, qs, ks, vs):
    index = at[0]
    sets = 4 - index // 4
    for n, ref in enumerate((q0, q1, q2, q3)):
        qs[pl.ds(n * BLOCK, BLOCK), :] = ref[...]
    for n, ref in enumerate((kv0, kv1, kv3)):
        ks[pl.ds(n * BLOCK, BLOCK), :] = ref[0:BLOCK, :]
        put_values(vs, n * BLOCK, ref[BLOCK : 2 * BLOCK, :])
    more = jnp.where(index >= 3, 3, jnp.where(index >= 1, 2, 1))
    row = lax.broadcasted_iota(jnp.int32, (TILE, CHUNK), 0)
    col = lax.broadcasted_iota(jnp.int32, (TILE, CHUNK), 1)
    ahead = col - row
    lane = lax.broadcasted_iota(jnp.int32, (TILE, LANES), 1)

    def keep(rows, state):
        top, total, acc = state
        acc_ref[rows, :] = acc
        ml_ref[rows, :] = jnp.where(lane < LANES // 2, top, total)

    def fast(first, causal):
        rows = [pl.ds(pl.multiple_of(first + u * TILE, TILE), TILE) for u in range(UNROLL)]
        every = []
        for u in range(UNROLL):
            scores = []
            for c in range(0, 3 * BLOCK, CHUNK):
                s = scores_of(qs[rows[u], :], ks[c : c + CHUNK, :])
                if causal and c < BLOCK:
                    s = jnp.where(ahead <= u * TILE - c, s, NEG)
                scores.append(s)
            every.append(scores)
        values = [vs[c : c + CHUNK, :] for c in range(0, 3 * BLOCK, CHUNK)]
        for u in range(UNROLL):
            keep(rows[u], one_pass(every[u], values, scale))

    @pl.when(index >= 3)
    def _():
        fast(0, True)

        def step(t, _):
            fast(t * BLOCK, False)
            return 0

        lax.fori_loop(1, sets, step, 0)

    @pl.when(index < 3)
    def _():
        def tile(t, _):
            rows = pl.ds(pl.multiple_of(t * TILE, TILE), TILE)
            q = qs[rows, :]
            limit = jnp.where(t < BLOCK // TILE, t * TILE, 4 * BLOCK)
            start = (
                jnp.full((TILE, 1), NEG, jnp.float32),
                jnp.zeros((TILE, LANES), jnp.float32),
                jnp.zeros((TILE, LANES), jnp.float32),
            )

            def block(b, carried):
                first = pl.multiple_of(b * CHUNK, CHUNK)
                keys = pl.ds(first, CHUNK)
                scores = scores_of(q, ks[keys, :])
                scores = jnp.where((ahead <= limit - first) | (first >= BLOCK), scores, NEG)
                return fold(carried, scores, vs[keys, :], scale)

            keep(rows, lax.fori_loop(0, more * (BLOCK // CHUNK), block, start))
            return 0

        lax.fori_loop(0, sets * (BLOCK // TILE), tile, 0)


def late_kernel(scale, at, q0, q1, q2, q3, g0, g1, g2, g3, k2, v2, acc_ref, ml_ref, own_ref, s0, s1, s2, s3, o1, o2, o3, qs, gs, os, ss, vs):
    index = at[0]
    sets = 4 - index // 4
    for n, ref in enumerate((q0, q1, q2, q3)):
        qs[pl.ds(n * BLOCK, BLOCK), :] = ref[...]
    for n, ref in enumerate((g0, g1, g2, g3)):
        gs[pl.ds(n * BLOCK, BLOCK), :] = ref[...]
    put_values(vs, 0, v2[...])
    lane = lax.broadcasted_iota(jnp.int32, (TILE, LANES), 1)
    groups = TILE // LANES

    def finish(number, rows, state):
        top, total, acc = state
        out = acc / total
        os[rows, :] = out
        dots = jnp.sum(gs[rows, :].astype(jnp.float32) * out, axis=1, keepdims=True)
        both = jnp.where(lane < LANES // 2, top + jnp.log2(total), dots)
        for g in range(groups):
            turned = both[g * LANES : (g + 1) * LANES, :].T
            ss[pl.ds(number * groups + g, 1), :] = turned[0:1, :]
            ss[pl.ds(4 * ROWS + number * groups + g, 1), :] = turned[LANES // 2 : LANES // 2 + 1, :]

    def before(rows):
        ml = ml_ref[rows, :]
        return ml[:, 0:1], ml[:, LANES // 2 : LANES // 2 + 1], acc_ref[rows, :]

    def step(t, _):
        numbers = [t * UNROLL + u for u in range(UNROLL)]
        rows = [pl.ds(pl.multiple_of(n * TILE, TILE), TILE) for n in numbers]

        @pl.when(index >= 2)
        def _():
            every = [
                [scores_of(qs[r, :], k2[c : c + CHUNK, :]) for c in range(0, BLOCK, CHUNK)]
                for r in rows
            ]
            values = [vs[c : c + CHUNK, :] for c in range(0, BLOCK, CHUNK)]
            for n, r, scores in zip(numbers, rows, every):
                finish(n, r, one_pass(scores, values, scale, before(r)))

        @pl.when(index < 2)
        def _():
            for n, r in zip(numbers, rows):
                finish(n, r, before(r))

        return 0

    lax.fori_loop(0, sets * (BLOCK // TILE) // UNROLL, step, 0)
    own_ref[...] = os[0:BLOCK, :]
    for n, (sref, oref) in enumerate(((s0, None), (s1, o1), (s2, o2), (s3, o3))):

        @pl.when(n < sets)
        def _():
            sref[0:ROWS, :] = ss[n * ROWS : (n + 1) * ROWS, :]
            sref[ROWS : 2 * ROWS, :] = ss[(4 + n) * ROWS : (5 + n) * ROWS, :]
            if oref is not None:
                oref[...] = os[n * BLOCK : (n + 1) * BLOCK, :].astype(jnp.bfloat16)

        @pl.when(n >= sets)
        def _():
            sref[...] = jnp.zeros_like(sref)
            if oref is not None:
                oref[...] = jnp.zeros_like(oref)


def near_kernel(scale, per_pos, positions, unroll, with_dot, at, q, kv0, kv1, k2, v2, sinks, *rest):
    if with_dot:
        grad, out_ref, dot_ref, ks, vs, fk, fv = rest
    else:
        out_ref, ks, vs, fk, fv = rest
    index = at[0]
    ks[0:BLOCK, :] = k2[...]
    put_values(vs, 0, v2[...])
    for n, ref in ((1, kv1), (2, kv0)):
        ks[n * BLOCK : (n + 1) * BLOCK, :] = ref[0:BLOCK, :]
        put_values(vs, n * BLOCK, ref[BLOCK : 2 * BLOCK, :])
    blank = jnp.zeros((LANES - SINK, LANES), jnp.bfloat16)
    fk[0:SINK, :] = sinks[0:SINK, :]
    fk[SINK:LANES, :] = blank
    put_values(fv, 0, sinks[SINK : 2 * SINK, :])
    put_values(fv, SINK, blank)
    tile = positions * per_pos
    width = WINDOW + positions
    row = lax.broadcasted_iota(jnp.int32, (tile, positions), 0) // per_pos
    col = lax.broadcasted_iota(jnp.int32, (tile, positions), 1)
    sink_row = lax.broadcasted_iota(jnp.int32, (tile, LANES), 0) // per_pos
    sink_col = lax.broadcasted_iota(jnp.int32, (tile, LANES), 1)
    first = (2 - index) * BLOCK
    cuts = [0, *range(positions, WINDOW, CHUNK), WINDOW, width]

    def group(t, partial_window):
        every, rows, begins = [], [], []
        for u in range(unroll):
            number = t * unroll + u
            rows.append(pl.ds(pl.multiple_of(number * tile, tile), tile))
            begin = pl.multiple_of(number * positions, positions)
            begins.append(begin)
            query = q[rows[u], :]
            scores = []
            for low, high in zip(cuts, cuts[1:]):
                s = scores_of(query, ks[pl.ds(pl.multiple_of(begin + low, LANES), high - low), :])
                if partial_window:
                    column = lax.broadcasted_iota(jnp.int32, (1, high - low), 1) + begin + low
                    s = s + jnp.where(column >= first, 0.0, NEG)
                if low == 0:
                    s = jnp.where(col > row, s, NEG)
                if low == WINDOW:
                    s = jnp.where(col <= row, s, NEG)
                scores.append(s)
            far = scores_of(query, fk[...])
            reach = index * BLOCK + begin + sink_row - sink_col
            scores.append(jnp.where((sink_col < SINK) & (reach >= WINDOW), far, NEG))
            every.append(scores)
        for u in range(unroll):
            values = [
                vs[pl.ds(pl.multiple_of(begins[u] + low, LANES), high - low), :]
                for low, high in zip(cuts, cuts[1:])
            ]
            _, total, acc = one_pass(every[u], values + [fv[...]], scale)
            out = acc / total
            out_ref[rows[u], :] = out.astype(out_ref.dtype)
            if with_dot:
                dot_ref[...] += jnp.sum(
                    grad[rows[u], :].astype(jnp.float32) * out, axis=0, keepdims=True
                )

    if with_dot:
        dot_ref[...] = jnp.zeros_like(dot_ref)
    for cond, partial_window in ((index >= 2, False), (index < 2, True)):

        @pl.when(cond)
        def _():
            def step(t, _):
                group(t, partial_window)
                return 0

            lax.fori_loop(0, BLOCK // (positions * unroll), step, 0)


def gate_kernel(norm, at, s0, s1, s2, s3, dot, row_ref):
    level = at[0] // 4
    logs, dots = [s0[0:ROWS, :]], [s0[ROWS : 2 * ROWS, :]]
    for n, ref in ((1, s1), (2, s2), (3, s3)):
        logs.append(jnp.where(level >= n, ref[0:ROWS, :], NEG))
        dots.append(ref[ROWS : 2 * ROWS, :])
    top = functools.reduce(jnp.maximum, logs)
    shares = [jnp.exp2(x - top) for x in logs]
    full = functools.reduce(jnp.add, [s * d for s, d in zip(shares, dots)])
    full = full / functools.reduce(jnp.add, shares)
    lanes = jnp.sum(full, axis=0, keepdims=True) - dot[0:1, :]
    value = jnp.sum(lanes, axis=1, keepdims=True) * norm
    lane = lax.broadcasted_iota(jnp.int32, row_ref.shape, 1)
    row_ref[...] = jnp.where(lane == at[1], value, 0.0)


def merge_kernel(at, gate, own, s0, s1, s2, s3, o1, o2, o3, near, mix_ref):
    level = at[0] // 4
    gated = gate[0]
    logs = [s0[0:ROWS, :]]
    for n, ref in ((1, s1), (2, s2), (3, s3)):
        logs.append(jnp.where(level >= n, ref[0:ROWS, :], NEG))
    top = functools.reduce(jnp.maximum, logs)
    shares = [jnp.exp2(x - top) for x in logs]
    whole = functools.reduce(jnp.add, shares)
    shares = [x / whole for x in shares]
    for g in range(BLOCK // LANES):
        rows = slice(g * LANES, (g + 1) * LANES)
        columns = [jnp.broadcast_to(x[g : g + 1, :], (LANES, LANES)).T for x in shares]
        full = columns[0] * own[rows, :]
        for column, ref in zip(columns[1:], (o1, o2, o3)):
            full = full + column * ref[rows, :].astype(jnp.float32)
        mix_ref[rows, :] = (gated * full + (1.0 - gated) * near[rows, :]).astype(jnp.bfloat16)


def call(kernel, scalars, arrays, outs, scratch, estimate):
    specs = [pl.BlockSpec(memory_space=pltpu.SMEM)] * len(scalars)
    specs += [pl.BlockSpec(memory_space=VMEM)] * len(arrays)
    return pl.pallas_call(
        kernel,
        out_shape=outs,
        in_specs=specs,
        out_specs=[pl.BlockSpec(memory_space=VMEM)] * len(outs),
        scratch_shapes=scratch,
        compiler_params=params(),
        cost_estimate=estimate,
    )(*scalars, *arrays)


def shape(rows, dtype):
    return jax.ShapeDtypeStruct((rows, LANES), dtype)


def on_device(query_states, key_states, value_states, gate_values, head_flags, output_grad):
    bf16, f32 = jnp.bfloat16, jnp.float32
    heads = head_flags.shape[0]
    ctx = lax.axis_size("ctx")
    index = lax.axis_index("ctx")
    scale = LOG2E / math.sqrt(LANES)
    keys = key_states.reshape(BLOCK, LANES)
    values = value_states.reshape(BLOCK, LANES)
    marked = (head_flags == 1)[None, :, None]
    which = jnp.sum(head_flags * jnp.arange(heads, dtype=jnp.int32))

    def pick(array):
        return jnp.sum(jnp.where(marked, array[0].astype(f32), 0.0), axis=1).astype(bf16)

    def ring(block, shift):
        return lax.ppermute(block, "ctx", [(i, (i + shift) % ctx) for i in range(ctx)])

    def down(block, n):
        return lax.ppermute(block, "ctx", [(i, i - 4 * n) for i in range(4 * n, ctx)])

    def home(block, n):
        return lax.ppermute(block, "ctx", [(i - 4 * n, i) for i in range(4 * n, ctx)])

    trips = range(1, DEPTH + 1)
    kv0 = jnp.concatenate([keys, values], axis=0)
    kv1, kv3 = ring(kv0, 1), ring(kv0, 3)

    def sinks_of(kv):
        return jnp.concatenate([kv[:SINK], kv[BLOCK : BLOCK + SINK]], axis=0)

    def after(array, *others):
        return lax.optimization_barrier((array, others))[0]

    middle = ctx // 2
    sinks = lax.ppermute(sinks_of(kv0), "ctx", [(0, middle)])
    query, grad = pick(query_states), pick(output_grad)
    query = after(query, sinks)
    visitors = [down(query, n) for n in trips]
    k2, v2 = ring(kv1[:BLOCK], 1), ring(kv3[BLOCK:], -1)
    grad = after(grad, *visitors)
    grads = [down(grad, n) for n in trips]
    at = jnp.stack([index, lax.axis_index("head") * heads + which]).astype(jnp.int32)
    gate = jnp.sum(jnp.where(head_flags == 1, gate_values, 0.0))[None]

    full_rows = (DEPTH + 1) * BLOCK
    acc, ml = call(
        functools.partial(early_kernel, scale),
        [at],
        [query, *visitors, kv0, kv1, kv3],
        [shape(full_rows, f32)] * 2,
        [
            VMEM((full_rows, LANES), bf16),
            VMEM((3 * BLOCK, LANES), bf16),
            VMEM((3 * BLOCK, 2 * LANES), bf16),
        ],
        cost(12),
    )
    late = call(
        functools.partial(late_kernel, scale),
        [at],
        [query, *visitors, grad, *grads, k2, v2, acc, ml],
        [shape(BLOCK, f32)] + [shape(2 * ROWS, f32)] * (DEPTH + 1) + [shape(BLOCK, bf16)] * DEPTH,
        [
            VMEM((full_rows, LANES), bf16),
            VMEM((full_rows, LANES), bf16),
            VMEM((full_rows, LANES), f32),
            VMEM((8 * ROWS, LANES), f32),
            VMEM((BLOCK, 2 * LANES), bf16),
        ],
        cost(4),
    )
    own, stats = late[0], late[1 : DEPTH + 2]
    sinks = jnp.where(index == 0, sinks_of(kv0), sinks)
    for place, kv in ((1, kv1), (2, jnp.concatenate([k2, v2], axis=0)), (3, kv3)):
        sinks = jnp.where(index == place, sinks_of(kv), sinks)
    letter = sinks.astype(f32)
    letters = [home(jnp.concatenate([stats[n], letter], axis=0), n) for n in trips]
    level = index // 4
    for n, got in zip(trips, letters):
        sinks = jnp.where((level == n) & (index != middle), got[2 * ROWS :].astype(bf16), sinks)
    stats = [stats[0], *letters]
    window = [kv0, kv1, k2, v2, sinks]
    scratch = [
        VMEM((3 * BLOCK, LANES), bf16),
        VMEM((3 * BLOCK, 2 * LANES), bf16),
        VMEM((LANES, LANES), bf16),
        VMEM((LANES, 2 * LANES), bf16),
    ]
    near_one, near_dot = call(
        functools.partial(near_kernel, scale, 1, 256, 4, True),
        [at],
        [query, *window, grad],
        [shape(BLOCK, f32), shape(ROWS, f32)],
        scratch,
        cost(2.5),
    )
    norm = 1.0 / math.sqrt(lax.axis_size("dp") * BLOCK * ctx * LANES)
    devices = lax.axis_size("dp") * lax.axis_size("head") * ctx
    [row] = call(
        functools.partial(gate_kernel, norm),
        [at],
        [*stats, near_dot],
        [shape(devices, f32)],
        [],
        cost(0.01, 2**17),
    )
    everyone = lax.all_to_all(row, ("dp", "head", "ctx"), 0, 0, tiled=True)
    gate_grad = jnp.sum(everyone, axis=0)[: heads * lax.axis_size("head")]
    outs = late[DEPTH + 2 :]
    outs = [home(part, n) for n, part in zip(trips, outs)]
    query_states, _ = lax.optimization_barrier((query_states, row))
    [near_all] = call(
        functools.partial(near_kernel, scale, heads, 128, 2, False),
        [at],
        [query_states.reshape(BLOCK * heads, LANES), *window],
        [shape(BLOCK * heads, bf16)],
        scratch,
        cost(9),
    )
    [mixed] = call(
        merge_kernel,
        [at, gate],
        [own, *stats, *outs, near_one],
        [shape(BLOCK, bf16)],
        [],
        cost(0.1),
    )
    near_all = near_all.reshape(1, BLOCK, heads, LANES)
    blended = jnp.where(marked[None], mixed[None, :, None, :], near_all)
    return (blended, gate_grad)


def solution(mesh):
    spec = P("dp", "ctx", "head", None)
    return jax.shard_map(
        on_device,
        mesh=mesh,
        in_specs=(spec, spec, spec, P("head"), P("head"), spec),
        out_specs=(spec, P()),
        check_vma=False,
    )
```

```python
import functools
import math

import jax
import jax.numpy as jnp
from jax import lax
from jax.experimental import pallas as pl
from jax.experimental.pallas import tpu as pltpu
from jax.sharding import PartitionSpec as P

SINK = 64
WINDOW = 2048
BLOCK = 1024
TILE = 512
UNROLL = 2
CHUNK = 512
ROWS = 8
DEPTH = 3
LANES = 128
VMEM = pltpu.VMEM
LOG2E = 1.4426950408889634
NEG = -1e30


def params():
    return pltpu.CompilerParams(vmem_limit_bytes=44 * 2**20)


def cost(units, bytes_accessed=4 * 2**20):
    return pl.CostEstimate(
        flops=int(units * 4 * BLOCK * BLOCK * LANES),
        bytes_accessed=bytes_accessed,
        transcendentals=int(units * BLOCK * BLOCK),
    )


def scores_of(q, k):
    return lax.dot_general(q, k, (((1,), (1,)), ((), ())), preferred_element_type=jnp.float32)


def fold(carried, scores, values, scale):
    top, total, acc = carried
    newest = jnp.maximum(top, jnp.max(scores, axis=1, keepdims=True) * scale)
    weights = jnp.exp2(scores * scale - newest).astype(jnp.bfloat16)
    factor = jnp.exp2(top - newest)
    update = jnp.dot(weights, values, preferred_element_type=jnp.float32)
    return newest, total * factor + update[:, LANES:], acc * factor + update[:, :LANES]


def one_pass(scores, values, scale, before=None):
    top = functools.reduce(
        jnp.maximum, [jnp.max(s, axis=1, keepdims=True) for s in scores]
    ) * scale
    if before is not None:
        top = jnp.maximum(top, before[0])
    update = functools.reduce(
        jnp.add,
        [
            jnp.dot(
                jnp.exp2(s * scale - top).astype(jnp.bfloat16),
                v(),
                preferred_element_type=jnp.float32,
            )
            for s, v in zip(scores, values)
        ],
    )
    total, acc = update[:, LANES:], update[:, :LANES]
    if before is not None:
        factor = jnp.exp2(before[0] - top)
        total = total + before[1] * factor
        acc = acc + before[2] * factor
    return top, total, acc


def take(ref, first, count):
    return ref[pl.ds(first, count), :]


def put_values(dest, first, source):
    rows = source.shape[0]
    dest[pl.ds(first, rows), 0:LANES] = source
    dest[pl.ds(first, rows), LANES : 2 * LANES] = jnp.ones((rows, LANES), jnp.bfloat16)


def pick_kernel(at, q, g, query_ref, grad_ref):
    heads = q.shape[0] // BLOCK
    rows = 2 * LANES
    row = lax.broadcasted_iota(jnp.int32, (rows, heads * rows), 0)
    col = lax.broadcasted_iota(jnp.int32, (rows, heads * rows), 1)
    chosen = jnp.where(col == heads * row + at[2], 1.0, 0.0).astype(jnp.bfloat16)
    for source, dest in ((q, query_ref), (g, grad_ref)):
        for n in range(BLOCK // rows):
            part = source[n * heads * rows : (n + 1) * heads * rows, :]
            moved = jnp.dot(chosen, part, preferred_element_type=jnp.float32)
            dest[n * rows : (n + 1) * rows, :] = moved.astype(jnp.bfloat16)


def early_kernel(scale, at, q0, q1, q2, q3, kv0, kv1, kv3, acc_ref, ml_ref, qs, ks, vs):
    index = at[0]
    sets = 4 - index // 4
    for n, ref in enumerate((q0, q1, q2, q3)):
        qs[pl.ds(n * BLOCK, BLOCK), :] = ref[...]
    for n, ref in enumerate((kv0, kv1, kv3)):
        ks[pl.ds(n * BLOCK, BLOCK), :] = ref[0:BLOCK, :]
        put_values(vs, n * BLOCK, ref[BLOCK : 2 * BLOCK, :])
    more = jnp.where(index >= 3, 3, jnp.where(index >= 1, 2, 1))
    row = lax.broadcasted_iota(jnp.int32, (TILE, CHUNK), 0)
    col = lax.broadcasted_iota(jnp.int32, (TILE, CHUNK), 1)
    ahead = col - row
    lane = lax.broadcasted_iota(jnp.int32, (TILE, LANES), 1)

    def keep(rows, state):
        top, total, acc = state
        acc_ref[rows, :] = acc
        ml_ref[rows, :] = jnp.where(lane < LANES // 2, top, total)

    def fast(first, causal):
        rows = [pl.ds(pl.multiple_of(first + u * TILE, TILE), TILE) for u in range(UNROLL)]
        every = []
        for u in range(UNROLL):
            scores = []
            for c in range(0, 3 * BLOCK, CHUNK):
                s = scores_of(qs[rows[u], :], ks[c : c + CHUNK, :])
                if causal and c < BLOCK:
                    s = jnp.where(ahead <= u * TILE - c, s, NEG)
                scores.append(s)
            every.append(scores)
        values = [functools.partial(take, vs, c, CHUNK) for c in range(0, 3 * BLOCK, CHUNK)]
        for u in range(UNROLL):
            keep(rows[u], one_pass(every[u], values, scale))

    @pl.when(index >= 3)
    def _():
        fast(0, True)

        def step(t, _):
            fast(t * BLOCK, False)
            return 0

        lax.fori_loop(1, sets, step, 0)

    @pl.when(index < 3)
    def _():
        def tile(t, _):
            rows = pl.ds(pl.multiple_of(t * TILE, TILE), TILE)
            q = qs[rows, :]
            limit = jnp.where(t < BLOCK // TILE, t * TILE, 4 * BLOCK)
            start = (
                jnp.full((TILE, 1), NEG, jnp.float32),
                jnp.zeros((TILE, LANES), jnp.float32),
                jnp.zeros((TILE, LANES), jnp.float32),
            )

            def block(b, carried):
                first = pl.multiple_of(b * CHUNK, CHUNK)
                keys = pl.ds(first, CHUNK)
                scores = scores_of(q, ks[keys, :])
                scores = jnp.where((ahead <= limit - first) | (first >= BLOCK), scores, NEG)
                return fold(carried, scores, vs[keys, :], scale)

            keep(rows, lax.fori_loop(0, more * (BLOCK // CHUNK), block, start))
            return 0

        lax.fori_loop(0, sets * (BLOCK // TILE), tile, 0)


def late_kernel(scale, at, q0, q1, q2, q3, g0, g1, g2, g3, k2, v2, acc_ref, ml_ref, own_ref, s0, s1, s2, s3, o1, o2, o3, vs):
    index = at[0]
    sets = 4 - index // 4
    put_values(vs, 0, v2[...])
    lane = lax.broadcasted_iota(jnp.int32, (TILE, LANES), 1)
    spot = lax.broadcasted_iota(jnp.int32, (2 * ROWS, LANES), 0) * (LANES // 16)
    chosen = jnp.where(lax.broadcasted_iota(jnp.int32, (2 * ROWS, LANES), 1) == spot, 1.0, 0.0)
    chosen = chosen.astype(jnp.bfloat16)
    groups = TILE // LANES

    def finish(u, state, grad, stat, dest):
        top, total, acc = state
        out = acc / total
        rows = slice(u * TILE, (u + 1) * TILE)
        dest[rows, :] = out.astype(dest.dtype)
        dots = jnp.sum(grad[rows, :].astype(jnp.float32) * out, axis=1, keepdims=True)
        rest = jnp.where(lane < LANES // 2, top + jnp.log2(total), dots)
        turned = jnp.zeros((2 * ROWS, TILE), jnp.float32)
        for _ in range(3):
            part = rest.astype(jnp.bfloat16)
            rest = rest - part.astype(jnp.float32)
            turned = turned + scores_of(chosen, part)
        for g in range(groups):
            lanes = slice(g * LANES, (g + 1) * LANES)
            spot = u * groups + g
            stat[spot : spot + 1, :] = turned[0:1, lanes]
            stat[ROWS + spot : ROWS + spot + 1, :] = turned[ROWS : ROWS + 1, lanes]

    def before(number):
        rows = slice(number * TILE, (number + 1) * TILE)
        ml = ml_ref[rows, :]
        return ml[:, 0:1], ml[:, LANES // 2 : LANES // 2 + 1], acc_ref[rows, :]

    for n, (query, grad, stat, dest) in enumerate(
        ((q0, g0, s0, own_ref), (q1, g1, s1, o1), (q2, g2, s2, o2), (q3, g3, s3, o3))
    ):

        @pl.when((index >= 2) & (n < sets))
        def _():
            every = [
                [
                    scores_of(query[u * TILE : (u + 1) * TILE, :], k2[c : c + CHUNK, :])
                    for c in range(0, BLOCK, CHUNK)
                ]
                for u in range(UNROLL)
            ]
            values = [functools.partial(take, vs, c, CHUNK) for c in range(0, BLOCK, CHUNK)]
            for u in range(UNROLL):
                state = one_pass(every[u], values, scale, before(n * UNROLL + u))
                finish(u, state, grad, stat, dest)

        @pl.when((index < 2) & (n < sets))
        def _():
            for u in range(UNROLL):
                finish(u, before(n * UNROLL + u), grad, stat, dest)

        @pl.when(n >= sets)
        def _():
            stat[...] = jnp.zeros_like(stat)
            dest[...] = jnp.zeros_like(dest)


def near_kernel(scale, per_pos, positions, unroll, with_dot, at, q, kv0, kv1, k2, v2, sinks, *rest):
    if with_dot:
        grad, out_ref, dot_ref, ks, vs, fk, fv = rest
    else:
        out_ref, ks, vs, fk, fv = rest
    index = at[0]
    ks[0:BLOCK, :] = k2[...]
    put_values(vs, 0, v2[...])
    for n, ref in ((1, kv1), (2, kv0)):
        ks[n * BLOCK : (n + 1) * BLOCK, :] = ref[0:BLOCK, :]
        put_values(vs, n * BLOCK, ref[BLOCK : 2 * BLOCK, :])
    blank = jnp.zeros((LANES - SINK, LANES), jnp.bfloat16)
    fk[0:SINK, :] = sinks[0:SINK, :]
    fk[SINK:LANES, :] = blank
    put_values(fv, 0, sinks[SINK : 2 * SINK, :])
    put_values(fv, SINK, blank)
    tile = positions * per_pos
    width = WINDOW + positions
    row = lax.broadcasted_iota(jnp.int32, (tile, positions), 0) // per_pos
    col = lax.broadcasted_iota(jnp.int32, (tile, positions), 1)
    sink_row = lax.broadcasted_iota(jnp.int32, (tile, LANES), 0) // per_pos
    sink_col = lax.broadcasted_iota(jnp.int32, (tile, LANES), 1)
    first = (2 - index) * BLOCK
    cuts = [0, *range(positions, WINDOW, CHUNK), WINDOW, width]

    def group(t, partial_window):
        every, rows, begins = [], [], []
        for u in range(unroll):
            number = t * unroll + u
            rows.append(pl.ds(pl.multiple_of(number * tile, tile), tile))
            begin = pl.multiple_of(number * positions, positions)
            begins.append(begin)
            query = q[rows[u], :]
            scores = []
            for low, high in zip(cuts, cuts[1:]):
                s = scores_of(query, ks[pl.ds(pl.multiple_of(begin + low, LANES), high - low), :])
                if partial_window:
                    column = lax.broadcasted_iota(jnp.int32, (1, high - low), 1) + begin + low
                    s = s + jnp.where(column >= first, 0.0, NEG)
                if low == 0:
                    s = jnp.where(col > row, s, NEG)
                if low == WINDOW:
                    s = jnp.where(col <= row, s, NEG)
                scores.append(s)
            far = scores_of(query, fk[...])
            reach = index * BLOCK + begin + sink_row - sink_col
            scores.append(jnp.where((sink_col < SINK) & (reach >= WINDOW), far, NEG))
            every.append(scores)
        for u in range(unroll):
            values = [
                functools.partial(take, vs, pl.multiple_of(begins[u] + low, LANES), high - low)
                for low, high in zip(cuts, cuts[1:])
            ]
            _, total, acc = one_pass(every[u], values + [functools.partial(take, fv, 0, LANES)], scale)
            out = acc / total
            out_ref[rows[u], :] = out.astype(out_ref.dtype)
            if with_dot:
                dot_ref[...] += jnp.sum(
                    grad[rows[u], :].astype(jnp.float32) * out, axis=0, keepdims=True
                )

    if with_dot:
        dot_ref[...] = jnp.zeros_like(dot_ref)
    for cond, partial_window in ((index >= 2, False), (index < 2, True)):

        @pl.when(cond)
        def _():
            def step(t, _):
                group(t, partial_window)
                return 0

            lax.fori_loop(0, BLOCK // (positions * unroll), step, 0)


def gate_kernel(norm, at, s0, s1, s2, s3, dot, row_ref):
    level = at[0] // 4
    logs, dots = [s0[0:ROWS, :]], [s0[ROWS : 2 * ROWS, :]]
    for n, ref in ((1, s1), (2, s2), (3, s3)):
        logs.append(jnp.where(level >= n, ref[0:ROWS, :], NEG))
        dots.append(ref[ROWS : 2 * ROWS, :])
    top = functools.reduce(jnp.maximum, logs)
    shares = [jnp.exp2(x - top) for x in logs]
    full = functools.reduce(jnp.add, [s * d for s, d in zip(shares, dots)])
    full = full / functools.reduce(jnp.add, shares)
    lanes = jnp.sum(full, axis=0, keepdims=True) - dot[0:1, :]
    value = jnp.sum(lanes, axis=1, keepdims=True) * norm
    lane = lax.broadcasted_iota(jnp.int32, row_ref.shape, 1)
    row_ref[...] = jnp.where(lane == at[1], value, 0.0)


def merge_kernel(at, gate, own, s0, s1, s2, s3, o1, o2, o3, near, mix_ref):
    level = at[0] // 4
    gated = gate[0]
    logs = [s0[0:ROWS, :]]
    for n, ref in ((1, s1), (2, s2), (3, s3)):
        logs.append(jnp.where(level >= n, ref[0:ROWS, :], NEG))
    top = functools.reduce(jnp.maximum, logs)
    shares = [jnp.exp2(x - top) for x in logs]
    whole = functools.reduce(jnp.add, shares)
    shares = [x / whole for x in shares]
    for g in range(BLOCK // LANES):
        rows = slice(g * LANES, (g + 1) * LANES)
        columns = [jnp.broadcast_to(x[g : g + 1, :], (LANES, LANES)).T for x in shares]
        full = columns[0] * own[rows, :]
        for column, ref in zip(columns[1:], (o1, o2, o3)):
            full = full + column * ref[rows, :].astype(jnp.float32)
        mix_ref[rows, :] = (gated * full + (1.0 - gated) * near[rows, :]).astype(jnp.bfloat16)


def call(kernel, scalars, arrays, outs, scratch, estimate):
    specs = [pl.BlockSpec(memory_space=pltpu.SMEM)] * len(scalars)
    specs += [pl.BlockSpec(memory_space=VMEM)] * len(arrays)
    return pl.pallas_call(
        kernel,
        out_shape=outs,
        in_specs=specs,
        out_specs=[pl.BlockSpec(memory_space=VMEM)] * len(outs),
        scratch_shapes=scratch,
        compiler_params=params(),
        cost_estimate=estimate,
    )(*scalars, *arrays)


def shape(rows, dtype):
    return jax.ShapeDtypeStruct((rows, LANES), dtype)


def on_device(query_states, key_states, value_states, gate_values, head_flags, output_grad):
    bf16, f32 = jnp.bfloat16, jnp.float32
    heads = head_flags.shape[0]
    ctx = lax.axis_size("ctx")
    index = lax.axis_index("ctx")
    scale = LOG2E / math.sqrt(LANES)
    keys = key_states.reshape(BLOCK, LANES)
    values = value_states.reshape(BLOCK, LANES)
    marked = (head_flags == 1)[None, :, None]
    which = jnp.sum(head_flags * jnp.arange(heads, dtype=jnp.int32))

    at = jnp.stack([index, lax.axis_index("head") * heads + which, which]).astype(jnp.int32)

    def ring(block, shift):
        return lax.ppermute(block, "ctx", [(i, (i + shift) % ctx) for i in range(ctx)])

    def down(block, n):
        return lax.ppermute(block, "ctx", [(i, i - 4 * n) for i in range(4 * n, ctx)])

    def home(block, n):
        return lax.ppermute(block, "ctx", [(i - 4 * n, i) for i in range(4 * n, ctx)])

    trips = range(1, DEPTH + 1)
    kv0 = jnp.concatenate([keys, values], axis=0)
    kv1, kv3 = ring(kv0, 1), ring(kv0, 3)

    def sinks_of(kv):
        return jnp.concatenate([kv[:SINK], kv[BLOCK : BLOCK + SINK]], axis=0)

    def after(array, *others):
        return lax.optimization_barrier((array, others))[0]

    flat = [a.reshape(BLOCK * heads, LANES) for a in (query_states, output_grad)]
    query, grad = call(pick_kernel, [at], flat, [shape(BLOCK, bf16)] * 2, [], cost(20))
    visitors = [down(query, n) for n in trips]
    k2, v2 = ring(kv1[:BLOCK], 1), ring(kv3[BLOCK:], -1)
    grad = after(grad, *visitors)
    grads = [down(grad, n) for n in trips]
    gate = jnp.sum(jnp.where(head_flags == 1, gate_values, 0.0))[None]

    full_rows = (DEPTH + 1) * BLOCK
    acc, ml = call(
        functools.partial(early_kernel, scale),
        [at],
        [query, *visitors, kv0, kv1, kv3],
        [shape(full_rows, f32)] * 2,
        [
            VMEM((full_rows, LANES), bf16),
            VMEM((3 * BLOCK, LANES), bf16),
            VMEM((3 * BLOCK, 2 * LANES), bf16),
        ],
        cost(12),
    )
    late = call(
        functools.partial(late_kernel, scale),
        [at],
        [query, *visitors, grad, *grads, k2, v2, acc, ml],
        [shape(BLOCK, f32)] + [shape(2 * ROWS, f32)] * (DEPTH + 1) + [shape(BLOCK, bf16)] * DEPTH,
        [VMEM((BLOCK, 2 * LANES), bf16)],
        cost(4),
    )
    own, stats = late[0], late[1 : DEPTH + 2]
    sinks = sinks_of(kv0)
    for place, kv in ((1, kv1), (2, jnp.concatenate([k2, v2], axis=0)), (3, kv3)):
        sinks = jnp.where(index == place, sinks_of(kv), sinks)
    letter = sinks.astype(f32)
    letters = [home(jnp.concatenate([stats[n], letter], axis=0), n) for n in trips]
    level = index // 4
    for n, got in zip(trips, letters):
        sinks = jnp.where(level == n, got[2 * ROWS :].astype(bf16), sinks)
    stats = [stats[0], *letters]
    window = [kv0, kv1, k2, v2, sinks]
    scratch = [
        VMEM((3 * BLOCK, LANES), bf16),
        VMEM((3 * BLOCK, 2 * LANES), bf16),
        VMEM((LANES, LANES), bf16),
        VMEM((LANES, 2 * LANES), bf16),
    ]
    near_one, near_dot = call(
        functools.partial(near_kernel, scale, 1, 256, 4, True),
        [at],
        [query, *window, grad],
        [shape(BLOCK, f32), shape(ROWS, f32)],
        scratch,
        cost(2.5),
    )
    norm = 1.0 / math.sqrt(lax.axis_size("dp") * BLOCK * ctx * LANES)
    devices = lax.axis_size("dp") * lax.axis_size("head") * ctx
    [row] = call(
        functools.partial(gate_kernel, norm),
        [at],
        [*stats, near_dot],
        [shape(devices, f32)],
        [],
        cost(0.01, 2**17),
    )
    everyone = lax.all_to_all(row, ("dp", "head", "ctx"), 0, 0, tiled=True)
    gate_grad = jnp.sum(everyone, axis=0)[: heads * lax.axis_size("head")]
    outs = late[DEPTH + 2 :]
    outs = [home(part, n) for n, part in zip(trips, outs)]
    query_states, _ = lax.optimization_barrier((query_states, row))
    [near_all] = call(
        functools.partial(near_kernel, scale, heads, 128, 2, False),
        [at],
        [query_states.reshape(BLOCK * heads, LANES), *window],
        [shape(BLOCK * heads, bf16)],
        scratch,
        cost(9),
    )
    [mixed] = call(
        merge_kernel,
        [at, gate],
        [own, *stats, *outs, near_one],
        [shape(BLOCK, bf16)],
        [],
        cost(0.1),
    )
    near_all = near_all.reshape(1, BLOCK, heads, LANES)
    blended = jnp.where(marked[None], mixed[None, :, None, :], near_all)
    return (blended, gate_grad)


def solution(mesh):
    spec = P("dp", "ctx", "head", None)
    return jax.shard_map(
        on_device,
        mesh=mesh,
        in_specs=(spec, spec, spec, P("head"), P("head"), spec),
        out_specs=(spec, P()),
        check_vma=False,
    )
```

```python
import functools
import math

import jax
import jax.numpy as jnp
from jax import lax
from jax.experimental import pallas as pl
from jax.experimental.pallas import tpu as pltpu
from jax.sharding import PartitionSpec as P

SINK = 64
WINDOW = 2048
BLOCK = 1024
TILE = 512
UNROLL = 2
CHUNK = 512
ROWS = 8
TAIL = 32
DEPTH = 3
LANES = 128
VMEM = pltpu.VMEM
LOG2E = 1.4426950408889634
NEG = -1e30


def params():
    return pltpu.CompilerParams(vmem_limit_bytes=44 * 2**20)


def cost(units, bytes_accessed=4 * 2**20):
    return pl.CostEstimate(
        flops=int(units * 4 * BLOCK * BLOCK * LANES),
        bytes_accessed=bytes_accessed,
        transcendentals=int(units * BLOCK * BLOCK),
    )


def scores_of(q, k):
    return lax.dot_general(q, k, (((1,), (1,)), ((), ())), preferred_element_type=jnp.float32)


def one_pass(scores, values, scale, before=None):
    top = functools.reduce(
        jnp.maximum, [jnp.max(s, axis=1, keepdims=True) for s in scores]
    ) * scale
    if before is not None:
        top = jnp.maximum(top, before[0])
    update = functools.reduce(
        jnp.add,
        [
            jnp.dot(
                jnp.exp2(s * scale - top).astype(jnp.bfloat16),
                v(),
                preferred_element_type=jnp.float32,
            )
            for s, v in zip(scores, values)
        ],
    )
    total, acc = update[:, LANES:], update[:, :LANES]
    if before is not None:
        factor = jnp.exp2(before[0] - top)
        total = total + before[1] * factor
        acc = acc + before[2] * factor
    return top, total, acc


def take(ref, first, count):
    return ref[pl.ds(first, count), :]


def put_values(dest, first, source):
    rows = source.shape[0]
    dest[pl.ds(first, rows), 0:LANES] = source
    dest[pl.ds(first, rows), LANES : 2 * LANES] = jnp.ones((rows, LANES), jnp.bfloat16)


def pick_kernel(at, q, g, query_ref, grad_ref):
    rows, heads = query_ref.shape[0], q.shape[0] // query_ref.shape[0]
    row = lax.broadcasted_iota(jnp.int32, (rows, heads * rows), 0)
    col = lax.broadcasted_iota(jnp.int32, (rows, heads * rows), 1)
    chosen = jnp.where(col == heads * row + at[2], 1.0, 0.0).astype(jnp.bfloat16)
    for source, dest in ((q, query_ref), (g, grad_ref)):
        moved = jnp.dot(chosen, source[...], preferred_element_type=jnp.float32)
        dest[...] = moved.astype(jnp.bfloat16)


def pick(at, arrays, heads):
    rows = 2 * LANES
    return pl.pallas_call(
        pick_kernel,
        grid=(BLOCK // rows,),
        out_shape=[shape(BLOCK, jnp.bfloat16)] * 2,
        in_specs=[pl.BlockSpec(memory_space=pltpu.SMEM)]
        + [pl.BlockSpec((heads * rows, LANES), lambda n: (n, 0))] * 2,
        out_specs=[pl.BlockSpec((rows, LANES), lambda n: (n, 0))] * 2,
        compiler_params=params(),
        cost_estimate=cost(20),
    )(at, *arrays)


def early_kernel(scale, at, q0, q1, q2, q3, kv0, kv1, kv3, acc_ref, ml_ref, qs, ks, vs):
    index = at[0]
    sets = 4 - index // 4
    for n, ref in enumerate((q0, q1, q2, q3)):
        qs[pl.ds(n * BLOCK, BLOCK), :] = ref[...]
    for n, ref in enumerate((kv0, kv1, kv3)):
        ks[pl.ds(n * BLOCK, BLOCK), :] = ref[0:BLOCK, :]
        put_values(vs, n * BLOCK, ref[BLOCK : 2 * BLOCK, :])
    for n, least in ((1, 1), (2, 3)):

        @pl.when(index < least)
        def _():
            ks[n * BLOCK : (n + 1) * BLOCK, :] = kv0[0:BLOCK, :]
            vs[n * BLOCK : (n + 1) * BLOCK, :] = jnp.zeros((BLOCK, 2 * LANES), jnp.bfloat16)

    row = lax.broadcasted_iota(jnp.int32, (TILE, CHUNK), 0)
    col = lax.broadcasted_iota(jnp.int32, (TILE, CHUNK), 1)
    ahead = col - row
    lane = lax.broadcasted_iota(jnp.int32, (TILE, LANES), 1)

    def keep(rows, state):
        top, total, acc = state
        acc_ref[rows, :] = acc
        ml_ref[rows, :] = jnp.where(lane < LANES // 2, top, total)

    def fast(first, causal):
        rows = [pl.ds(pl.multiple_of(first + u * TILE, TILE), TILE) for u in range(UNROLL)]
        every = []
        for u in range(UNROLL):
            scores = []
            for c in range(0, 3 * BLOCK, CHUNK):
                s = scores_of(qs[rows[u], :], ks[c : c + CHUNK, :])
                if causal and c < BLOCK:
                    s = jnp.where(ahead <= u * TILE - c, s, NEG)
                elif causal:
                    s = jnp.where(index >= (1 if c < 2 * BLOCK else 3), s, NEG)
                scores.append(s)
            every.append(scores)
        values = [functools.partial(take, vs, c, CHUNK) for c in range(0, 3 * BLOCK, CHUNK)]
        for u in range(UNROLL):
            keep(rows[u], one_pass(every[u], values, scale))

    fast(0, True)

    def step(t, _):
        fast(t * BLOCK, False)
        return 0

    lax.fori_loop(1, sets, step, 0)


def late_kernel(scale, at, q0, q1, q2, q3, k2, v2, acc_ref, ml_ref, own_ref, lse_ref, p1, p2, p3, vs, tail):
    index = at[0]
    sets = 4 - index // 4
    put_values(vs, 0, v2[...])
    first = lax.broadcasted_iota(jnp.int32, (2 * ROWS, LANES), 1) == 0
    chosen = jnp.where(first, 1.0, 0.0).astype(jnp.bfloat16)
    groups = TILE // LANES

    def finish(u, state, dest):
        top, total, acc = state
        dest[u * TILE : (u + 1) * TILE, :] = (acc / total).astype(dest.dtype)
        rest = top + jnp.log2(total)
        for p in range(3):
            part = rest.astype(jnp.bfloat16)
            rest = rest - part.astype(jnp.float32)
            turned = scores_of(chosen, part)
            for g in range(groups):
                spot = p * ROWS + u * groups + g
                tail[spot : spot + 1, :] = turned[0:1, g * LANES : (g + 1) * LANES]

    def before(number):
        rows = slice(number * TILE, (number + 1) * TILE)
        ml = ml_ref[rows, :]
        return ml[:, 0:1], ml[:, LANES // 2 : LANES // 2 + 1], acc_ref[rows, :]

    tail[3 * ROWS : TAIL, :] = jnp.zeros((TAIL - 3 * ROWS, LANES), jnp.float32)
    for n, (query, dest) in enumerate(((q0, own_ref), (q1, p1), (q2, p2), (q3, p3))):

        @pl.when((index >= 2) & (n < sets))
        def _():
            every = [
                [
                    scores_of(query[u * TILE : (u + 1) * TILE, :], k2[c : c + CHUNK, :])
                    for c in range(0, BLOCK, CHUNK)
                ]
                for u in range(UNROLL)
            ]
            values = [functools.partial(take, vs, c, CHUNK) for c in range(0, BLOCK, CHUNK)]
            for u in range(UNROLL):
                finish(u, one_pass(every[u], values, scale, before(n * UNROLL + u)), dest)

        @pl.when((index < 2) & (n < sets))
        def _():
            for u in range(UNROLL):
                top, total, acc = before(n * UNROLL + u)
                finish(u, (top, jnp.broadcast_to(total, acc.shape), acc), dest)

        @pl.when(n < sets)
        def _():
            if n == 0:
                lse_ref[...] = tail[0:ROWS] + tail[ROWS : 2 * ROWS] + tail[2 * ROWS : 3 * ROWS]
            else:
                dest[BLOCK : BLOCK + TAIL, :] = tail[...].astype(jnp.bfloat16)

        @pl.when(n >= sets)
        def _():
            dest[...] = jnp.zeros_like(dest)


def near_kernel(scale, per_pos, positions, unroll, at, q, kv0, kv1, k2, v2, sinks, out_ref, ks, vs, fk, fv):
    index = at[0]
    ks[0:BLOCK, :] = k2[...]
    put_values(vs, 0, v2[...])
    for n, ref in ((1, kv1), (2, kv0)):
        ks[n * BLOCK : (n + 1) * BLOCK, :] = ref[0:BLOCK, :]
        put_values(vs, n * BLOCK, ref[BLOCK : 2 * BLOCK, :])
    blank = jnp.zeros((LANES - SINK, LANES), jnp.bfloat16)
    fk[0:SINK, :] = sinks[0:SINK, :]
    fk[SINK:LANES, :] = blank
    put_values(fv, 0, sinks[SINK : 2 * SINK, :])
    put_values(fv, SINK, blank)
    tile = positions * per_pos
    width = WINDOW + positions
    row = lax.broadcasted_iota(jnp.int32, (tile, positions), 0) // per_pos
    col = lax.broadcasted_iota(jnp.int32, (tile, positions), 1)
    sink_row = lax.broadcasted_iota(jnp.int32, (tile, LANES), 0) // per_pos
    sink_col = lax.broadcasted_iota(jnp.int32, (tile, LANES), 1)
    first = (2 - index) * BLOCK
    cuts = [0, *range(positions, WINDOW, CHUNK), WINDOW, width]

    def group(t, partial_window):
        every, rows, begins = [], [], []
        for u in range(unroll):
            number = t * unroll + u
            rows.append(pl.ds(pl.multiple_of(number * tile, tile), tile))
            begin = pl.multiple_of(number * positions, positions)
            begins.append(begin)
            query = q[rows[u], :]
            scores = []
            for low, high in zip(cuts, cuts[1:]):
                s = scores_of(query, ks[pl.ds(pl.multiple_of(begin + low, LANES), high - low), :])
                if partial_window:
                    column = lax.broadcasted_iota(jnp.int32, (1, high - low), 1) + begin + low
                    s = s + jnp.where(column >= first, 0.0, NEG)
                if low == 0:
                    s = jnp.where(col > row, s, NEG)
                if low == WINDOW:
                    s = jnp.where(col <= row, s, NEG)
                scores.append(s)
            far = scores_of(query, fk[...])
            reach = index * BLOCK + begin + sink_row - sink_col
            scores.append(jnp.where((sink_col < SINK) & (reach >= WINDOW), far, NEG))
            every.append(scores)
        for u in range(unroll):
            values = [
                functools.partial(take, vs, pl.multiple_of(begins[u] + low, LANES), high - low)
                for low, high in zip(cuts, cuts[1:])
            ]
            _, total, acc = one_pass(every[u], values + [functools.partial(take, fv, 0, LANES)], scale)
            out_ref[rows[u], :] = (acc / total).astype(out_ref.dtype)

    for cond, partial_window in ((index >= 2, False), (index < 2, True)):

        @pl.when(cond)
        def _():
            def step(t, _):
                group(t, partial_window)
                return 0

            lax.fori_loop(0, BLOCK // (positions * unroll), step, 0)


def merge_kernel(norm, at, gate, own, lse, p1, p2, p3, near, grad, mix_ref, row_ref):
    level = at[0] // 4
    gated = gate[0]
    logs = [lse[...]]
    for n, ref in ((1, p1), (2, p2), (3, p3)):
        tail = ref[BLOCK : BLOCK + TAIL, :].astype(jnp.float32)
        value = tail[0:ROWS] + tail[ROWS : 2 * ROWS] + tail[2 * ROWS : 3 * ROWS]
        logs.append(jnp.where(level >= n, value, NEG))
    top = functools.reduce(jnp.maximum, logs)
    shares = [jnp.exp2(x - top) for x in logs]
    whole = functools.reduce(jnp.add, shares)
    shares = [x / whole for x in shares]
    total = jnp.zeros((1, LANES), jnp.float32)
    for g in range(BLOCK // LANES):
        rows = slice(g * LANES, (g + 1) * LANES)
        columns = [jnp.broadcast_to(x[g : g + 1, :], (LANES, LANES)).T for x in shares]
        full = columns[0] * own[rows, :]
        for column, ref in zip(columns[1:], (p1, p2, p3)):
            full = full + column * ref[rows, :].astype(jnp.float32)
        close = near[rows, :]
        mix_ref[rows, :] = (gated * full + (1.0 - gated) * close).astype(jnp.bfloat16)
        total = total + jnp.sum(
            grad[rows, :].astype(jnp.float32) * (full - close), axis=0, keepdims=True
        )
    value = jnp.sum(total, axis=1, keepdims=True) * norm
    lane = lax.broadcasted_iota(jnp.int32, row_ref.shape, 1)
    row_ref[...] = jnp.where(lane == at[1], value, 0.0)


def call(kernel, scalars, arrays, outs, scratch, estimate):
    specs = [pl.BlockSpec(memory_space=pltpu.SMEM)] * len(scalars)
    specs += [pl.BlockSpec(memory_space=VMEM)] * len(arrays)
    return pl.pallas_call(
        kernel,
        out_shape=outs,
        in_specs=specs,
        out_specs=[pl.BlockSpec(memory_space=VMEM)] * len(outs),
        scratch_shapes=scratch,
        compiler_params=params(),
        cost_estimate=estimate,
    )(*scalars, *arrays)


def shape(rows, dtype):
    return jax.ShapeDtypeStruct((rows, LANES), dtype)


def on_device(query_states, key_states, value_states, gate_values, head_flags, output_grad):
    bf16, f32 = jnp.bfloat16, jnp.float32
    heads = head_flags.shape[0]
    ctx = lax.axis_size("ctx")
    index = lax.axis_index("ctx")
    scale = LOG2E / math.sqrt(LANES)
    keys = key_states.reshape(BLOCK, LANES)
    values = value_states.reshape(BLOCK, LANES)
    marked = (head_flags == 1)[None, :, None]
    which = jnp.sum(head_flags * jnp.arange(heads, dtype=jnp.int32))

    at = jnp.stack([index, lax.axis_index("head") * heads + which, which]).astype(jnp.int32)

    def ring(block, shift):
        return lax.ppermute(block, "ctx", [(i, (i + shift) % ctx) for i in range(ctx)])

    def down(block, n):
        return lax.ppermute(block, "ctx", [(i, i - 4 * n) for i in range(4 * n, ctx)])

    def home(block, n):
        return lax.ppermute(block, "ctx", [(i - 4 * n, i) for i in range(4 * n, ctx)])

    trips = range(1, DEPTH + 1)
    kv0 = jnp.concatenate([keys, values], axis=0)
    kv1, kv3 = ring(kv0, 1), ring(kv0, 3)

    def sinks_of(kv):
        return jnp.concatenate([kv[:SINK], kv[BLOCK : BLOCK + SINK]], axis=0)

    flat = [a.reshape(BLOCK * heads, LANES) for a in (query_states, output_grad)]
    query, grad = pick(at, flat, heads)
    visitors = [down(query, n) for n in trips]
    k2, v2 = ring(kv1[:BLOCK], 1), ring(kv3[BLOCK:], -1)
    gate = jnp.sum(jnp.where(head_flags == 1, gate_values, 0.0))[None]

    full_rows = (DEPTH + 1) * BLOCK
    acc, ml = call(
        functools.partial(early_kernel, scale),
        [at],
        [query, *visitors, kv0, kv1, kv3],
        [shape(full_rows, f32)] * 2,
        [
            VMEM((full_rows, LANES), bf16),
            VMEM((3 * BLOCK, LANES), bf16),
            VMEM((3 * BLOCK, 2 * LANES), bf16),
        ],
        cost(12),
    )
    sinks = sinks_of(kv0)
    for place, kv in ((1, kv1), (2, jnp.concatenate([k2, v2], axis=0)), (3, kv3)):
        sinks = jnp.where(index == place, sinks_of(kv), sinks)
    level = index // 4
    moved = [
        lax.ppermute(sinks, "ctx", [(i, i + 4 * n) for i in range(4)]) for n in trips
    ]
    for n, got in zip(trips, moved):
        sinks = jnp.where(level == n, got, sinks)
    own, lse, *parts = call(
        functools.partial(late_kernel, scale),
        [at],
        [query, *visitors, k2, v2, acc, ml],
        [shape(BLOCK, f32), shape(ROWS, f32)] + [shape(BLOCK + TAIL, bf16)] * DEPTH,
        [VMEM((BLOCK, 2 * LANES), bf16), VMEM((TAIL, LANES), f32)],
        cost(4),
    )
    parts = [home(part, n) for n, part in zip(trips, parts)]
    window = [kv0, kv1, k2, v2, sinks]
    scratch = [
        VMEM((3 * BLOCK, LANES), bf16),
        VMEM((3 * BLOCK, 2 * LANES), bf16),
        VMEM((LANES, LANES), bf16),
        VMEM((LANES, 2 * LANES), bf16),
    ]
    [near_one] = call(
        functools.partial(near_kernel, scale, 1, 256, 4),
        [at],
        [query, *window],
        [shape(BLOCK, f32)],
        scratch,
        cost(2.5),
    )
    [near_all] = call(
        functools.partial(near_kernel, scale, heads, 128, 2),
        [at],
        [flat[0], *window],
        [shape(BLOCK * heads, bf16)],
        scratch,
        cost(9),
    )
    norm = 1.0 / math.sqrt(lax.axis_size("dp") * BLOCK * ctx * LANES)
    devices = lax.axis_size("dp") * lax.axis_size("head") * ctx
    mixed, row = call(
        functools.partial(merge_kernel, norm),
        [at, gate],
        [own, lse, *parts, near_one, grad],
        [shape(BLOCK, bf16), shape(devices, f32)],
        [],
        cost(0.1),
    )
    everyone = lax.all_to_all(row, ("dp", "head", "ctx"), 0, 0, tiled=True)
    gate_grad = jnp.sum(everyone, axis=0)[: heads * lax.axis_size("head")]
    near_all = near_all.reshape(1, BLOCK, heads, LANES)
    blended = jnp.where(marked[None], mixed[None, :, None, :], near_all)
    return (blended, gate_grad)


def solution(mesh):
    spec = P("dp", "ctx", "head", None)
    return jax.shard_map(
        on_device,
        mesh=mesh,
        in_specs=(spec, spec, spec, P("head"), P("head"), spec),
        out_specs=(spec, P()),
        check_vma=False,
    )
```

```python
import functools
import math

import jax
import jax.numpy as jnp
from jax import lax
from jax.experimental import pallas as pl
from jax.experimental.pallas import tpu as pltpu
from jax.sharding import PartitionSpec as P

SINK = 64
WINDOW = 2048
BLOCK = 1024
TILE = 512
UNROLL = 2
CHUNK = 512
ROWS = 8
TAIL = 32
DEPTH = 3
LANES = 128
VMEM = pltpu.VMEM
LOG2E = 1.4426950408889634
NEG = -1e30


def params():
    return pltpu.CompilerParams(vmem_limit_bytes=44 * 2**20)


def cost(units, bytes_accessed=4 * 2**20):
    return pl.CostEstimate(
        flops=int(units * 4 * BLOCK * BLOCK * LANES),
        bytes_accessed=bytes_accessed,
        transcendentals=int(units * BLOCK * BLOCK),
    )


def scores_of(q, k):
    return lax.dot_general(q, k, (((1,), (1,)), ((), ())), preferred_element_type=jnp.float32)


def one_pass(scores, values, scale, before=None):
    top = functools.reduce(
        jnp.maximum, [jnp.max(s, axis=1, keepdims=True) for s in scores]
    ) * scale
    if before is not None:
        top = jnp.maximum(top, before[0])
    update = functools.reduce(
        jnp.add,
        [
            jnp.dot(
                jnp.exp2(s * scale - top).astype(jnp.bfloat16),
                v(),
                preferred_element_type=jnp.float32,
            )
            for s, v in zip(scores, values)
        ],
    )
    total, acc = update[:, LANES:], update[:, :LANES]
    if before is not None:
        factor = jnp.exp2(before[0] - top)
        total = total + before[1] * factor
        acc = acc + before[2] * factor
    return top, total, acc


def take(ref, first, count):
    return ref[pl.ds(first, count), :]


def put_values(dest, first, source):
    rows = source.shape[0]
    dest[pl.ds(first, rows), 0:LANES] = source
    dest[pl.ds(first, rows), LANES : 2 * LANES] = jnp.ones((rows, LANES), jnp.bfloat16)


def pick_kernel(at, q, g, query_ref, grad_ref):
    rows, heads = query_ref.shape[0], q.shape[0] // query_ref.shape[0]
    row = lax.broadcasted_iota(jnp.int32, (rows, heads * rows), 0)
    col = lax.broadcasted_iota(jnp.int32, (rows, heads * rows), 1)
    chosen = jnp.where(col == heads * row + at[2], 1.0, 0.0).astype(jnp.bfloat16)
    for source, dest in ((q, query_ref), (g, grad_ref)):
        moved = jnp.dot(chosen, source[...], preferred_element_type=jnp.float32)
        dest[...] = moved.astype(jnp.bfloat16)


def pick(at, arrays, heads):
    rows = 2 * LANES
    return pl.pallas_call(
        pick_kernel,
        grid=(BLOCK // rows,),
        out_shape=[shape(BLOCK, jnp.bfloat16)] * 2,
        in_specs=[pl.BlockSpec(memory_space=pltpu.SMEM)]
        + [pl.BlockSpec((heads * rows, LANES), lambda n: (n, 0))] * 2,
        out_specs=[pl.BlockSpec((rows, LANES), lambda n: (n, 0))] * 2,
        compiler_params=params(),
        cost_estimate=cost(20),
    )(at, *arrays)


def early_kernel(scale, at, q0, q1, q2, q3, kv0, k1, v1, kv3, acc_ref, ml_ref, qs, ks, vs):
    index = at[0]
    sets = 4 - index // 4
    for n, ref in enumerate((q0, q1, q2, q3)):
        qs[pl.ds(n * BLOCK, BLOCK), :] = ref[...]
    for n, ref in ((0, kv0), (2, kv3)):
        ks[pl.ds(n * BLOCK, BLOCK), :] = ref[0:BLOCK, :]
        put_values(vs, n * BLOCK, ref[BLOCK : 2 * BLOCK, :])
    ks[BLOCK : 2 * BLOCK, :] = k1[...]
    put_values(vs, BLOCK, v1[...])
    for n, least in ((1, 1), (2, 3)):

        @pl.when(index < least)
        def _():
            ks[n * BLOCK : (n + 1) * BLOCK, :] = kv0[0:BLOCK, :]
            vs[n * BLOCK : (n + 1) * BLOCK, :] = jnp.zeros((BLOCK, 2 * LANES), jnp.bfloat16)

    row = lax.broadcasted_iota(jnp.int32, (TILE, CHUNK), 0)
    col = lax.broadcasted_iota(jnp.int32, (TILE, CHUNK), 1)
    ahead = col - row
    lane = lax.broadcasted_iota(jnp.int32, (TILE, LANES), 1)

    def keep(rows, state):
        top, total, acc = state
        acc_ref[rows, :] = acc
        ml_ref[rows, :] = jnp.where(lane < LANES // 2, top, total)

    def fast(first, causal):
        rows = [pl.ds(pl.multiple_of(first + u * TILE, TILE), TILE) for u in range(UNROLL)]
        every = []
        for u in range(UNROLL):
            scores = []
            for c in range(0, 3 * BLOCK, CHUNK):
                s = scores_of(qs[rows[u], :], ks[c : c + CHUNK, :])
                if causal and c < BLOCK:
                    s = jnp.where(ahead <= u * TILE - c, s, NEG)
                elif causal:
                    s = jnp.where(index >= (1 if c < 2 * BLOCK else 3), s, NEG)
                scores.append(s)
            every.append(scores)
        values = [functools.partial(take, vs, c, CHUNK) for c in range(0, 3 * BLOCK, CHUNK)]
        for u in range(UNROLL):
            keep(rows[u], one_pass(every[u], values, scale))

    fast(0, True)

    def step(t, _):
        fast(t * BLOCK, False)
        return 0

    lax.fori_loop(1, sets, step, 0)


def late_kernel(scale, at, q0, q1, q2, q3, k2, v2, acc_ref, ml_ref, own_ref, lse_ref, p1, p2, p3, vs, tail):
    index = at[0]
    sets = 4 - index // 4
    put_values(vs, 0, v2[...])
    first = lax.broadcasted_iota(jnp.int32, (2 * ROWS, LANES), 1) == 0
    chosen = jnp.where(first, 1.0, 0.0).astype(jnp.bfloat16)
    groups = TILE // LANES

    def finish(u, state, dest):
        top, total, acc = state
        dest[u * TILE : (u + 1) * TILE, :] = (acc / total).astype(dest.dtype)
        rest = top + jnp.log2(total)
        for p in range(3):
            part = rest.astype(jnp.bfloat16)
            rest = rest - part.astype(jnp.float32)
            turned = scores_of(chosen, part)
            for g in range(groups):
                spot = p * ROWS + u * groups + g
                tail[spot : spot + 1, :] = turned[0:1, g * LANES : (g + 1) * LANES]

    def before(number):
        rows = slice(number * TILE, (number + 1) * TILE)
        ml = ml_ref[rows, :]
        return ml[:, 0:1], ml[:, LANES // 2 : LANES // 2 + 1], acc_ref[rows, :]

    tail[3 * ROWS : TAIL, :] = jnp.zeros((TAIL - 3 * ROWS, LANES), jnp.float32)
    for n, (query, dest) in enumerate(((q0, own_ref), (q1, p1), (q2, p2), (q3, p3))):

        @pl.when((index >= 2) & (n < sets))
        def _():
            every = [
                [
                    scores_of(query[u * TILE : (u + 1) * TILE, :], k2[c : c + CHUNK, :])
                    for c in range(0, BLOCK, CHUNK)
                ]
                for u in range(UNROLL)
            ]
            values = [functools.partial(take, vs, c, CHUNK) for c in range(0, BLOCK, CHUNK)]
            for u in range(UNROLL):
                finish(u, one_pass(every[u], values, scale, before(n * UNROLL + u)), dest)

        @pl.when((index < 2) & (n < sets))
        def _():
            for u in range(UNROLL):
                top, total, acc = before(n * UNROLL + u)
                finish(u, (top, jnp.broadcast_to(total, acc.shape), acc), dest)

        @pl.when(n < sets)
        def _():
            if n == 0:
                lse_ref[...] = tail[0:ROWS] + tail[ROWS : 2 * ROWS] + tail[2 * ROWS : 3 * ROWS]
            else:
                dest[BLOCK : BLOCK + TAIL, :] = tail[...].astype(jnp.bfloat16)

        @pl.when(n >= sets)
        def _():
            dest[...] = jnp.zeros_like(dest)


def near_kernel(scale, per_pos, positions, unroll, start, at, q, kv0, k1, v1, k2, v2, sinks, out_ref, ks, vs, fk, fv):
    index = at[0]
    ks[0:BLOCK, :] = k2[...]
    put_values(vs, 0, v2[...])
    ks[BLOCK : 2 * BLOCK, :] = k1[...]
    put_values(vs, BLOCK, v1[...])
    ks[2 * BLOCK : 3 * BLOCK, :] = kv0[0:BLOCK, :]
    put_values(vs, 2 * BLOCK, kv0[BLOCK : 2 * BLOCK, :])
    blank = jnp.zeros((LANES - SINK, LANES), jnp.bfloat16)
    fk[0:SINK, :] = sinks[0:SINK, :]
    fk[SINK:LANES, :] = blank
    put_values(fv, 0, sinks[SINK : 2 * SINK, :])
    put_values(fv, SINK, blank)
    tile = positions * per_pos
    width = WINDOW + positions
    row = lax.broadcasted_iota(jnp.int32, (tile, positions), 0) // per_pos
    col = lax.broadcasted_iota(jnp.int32, (tile, positions), 1)
    sink_row = lax.broadcasted_iota(jnp.int32, (tile, LANES), 0) // per_pos
    sink_col = lax.broadcasted_iota(jnp.int32, (tile, LANES), 1)
    first = (2 - index) * BLOCK
    cuts = [0, *range(positions, WINDOW, CHUNK), WINDOW, width]

    def group(t, partial_window):
        every, rows, begins = [], [], []
        for u in range(unroll):
            number = t * unroll + u
            rows.append(pl.ds(pl.multiple_of(number * tile, tile), tile))
            begin = pl.multiple_of(start + number * positions, positions)
            begins.append(begin)
            query = q[pl.ds(pl.multiple_of((start + number * positions) * per_pos, tile), tile), :]
            scores = []
            for low, high in zip(cuts, cuts[1:]):
                s = scores_of(query, ks[pl.ds(pl.multiple_of(begin + low, LANES), high - low), :])
                if partial_window:
                    column = lax.broadcasted_iota(jnp.int32, (1, high - low), 1) + begin + low
                    s = s + jnp.where(column >= first, 0.0, NEG)
                if low == 0:
                    s = jnp.where(col > row, s, NEG)
                if low == WINDOW:
                    s = jnp.where(col <= row, s, NEG)
                scores.append(s)
            far = scores_of(query, fk[...])
            reach = index * BLOCK + begin + sink_row - sink_col
            scores.append(jnp.where((sink_col < SINK) & (reach >= WINDOW), far, NEG))
            every.append(scores)
        for u in range(unroll):
            values = [
                functools.partial(take, vs, pl.multiple_of(begins[u] + low, LANES), high - low)
                for low, high in zip(cuts, cuts[1:])
            ]
            _, total, acc = one_pass(every[u], values + [functools.partial(take, fv, 0, LANES)], scale)
            out_ref[rows[u], :] = (acc / total).astype(out_ref.dtype)

    for cond, partial_window in ((index >= 2, False), (index < 2, True)):

        @pl.when(cond)
        def _():
            def step(t, _):
                group(t, partial_window)
                return 0

            lax.fori_loop(0, out_ref.shape[0] // (tile * unroll), step, 0)


def merge_kernel(norm, at, gate, own, lse, p1, p2, p3, near, grad, mix_ref, row_ref):
    level = at[0] // 4
    gated = gate[0]
    logs = [lse[...]]
    for n, ref in ((1, p1), (2, p2), (3, p3)):
        tail = ref[BLOCK : BLOCK + TAIL, :].astype(jnp.float32)
        value = tail[0:ROWS] + tail[ROWS : 2 * ROWS] + tail[2 * ROWS : 3 * ROWS]
        logs.append(jnp.where(level >= n, value, NEG))
    top = functools.reduce(jnp.maximum, logs)
    shares = [jnp.exp2(x - top) for x in logs]
    whole = functools.reduce(jnp.add, shares)
    shares = [x / whole for x in shares]
    total = jnp.zeros((1, LANES), jnp.float32)
    for g in range(BLOCK // LANES):
        rows = slice(g * LANES, (g + 1) * LANES)
        columns = [jnp.broadcast_to(x[g : g + 1, :], (LANES, LANES)).T for x in shares]
        full = columns[0] * own[rows, :]
        for column, ref in zip(columns[1:], (p1, p2, p3)):
            full = full + column * ref[rows, :].astype(jnp.float32)
        close = near[rows, :]
        mix_ref[rows, :] = (gated * full + (1.0 - gated) * close).astype(jnp.bfloat16)
        total = total + jnp.sum(
            grad[rows, :].astype(jnp.float32) * (full - close), axis=0, keepdims=True
        )
    value = jnp.sum(total, axis=1, keepdims=True) * norm
    lane = lax.broadcasted_iota(jnp.int32, row_ref.shape, 1)
    row_ref[...] = jnp.where(lane == at[1], value, 0.0)


def call(kernel, scalars, arrays, outs, scratch, estimate):
    specs = [pl.BlockSpec(memory_space=pltpu.SMEM)] * len(scalars)
    specs += [pl.BlockSpec(memory_space=VMEM)] * len(arrays)
    return pl.pallas_call(
        kernel,
        out_shape=outs,
        in_specs=specs,
        out_specs=[pl.BlockSpec(memory_space=VMEM)] * len(outs),
        scratch_shapes=scratch,
        compiler_params=params(),
        cost_estimate=estimate,
    )(*scalars, *arrays)


def shape(rows, dtype):
    return jax.ShapeDtypeStruct((rows, LANES), dtype)


def on_device(query_states, key_states, value_states, gate_values, head_flags, output_grad):
    bf16, f32 = jnp.bfloat16, jnp.float32
    heads = head_flags.shape[0]
    ctx = lax.axis_size("ctx")
    index = lax.axis_index("ctx")
    scale = LOG2E / math.sqrt(LANES)
    keys = key_states.reshape(BLOCK, LANES)
    values = value_states.reshape(BLOCK, LANES)
    marked = (head_flags == 1)[None, :, None]
    which = jnp.sum(head_flags * jnp.arange(heads, dtype=jnp.int32))

    at = jnp.stack([index, lax.axis_index("head") * heads + which, which]).astype(jnp.int32)

    def ring(block, shift):
        return lax.ppermute(block, "ctx", [(i, (i + shift) % ctx) for i in range(ctx)])

    def down(block, n):
        return lax.ppermute(block, "ctx", [(i, i - 4 * n) for i in range(4 * n, ctx)])

    def home(block, n):
        return lax.ppermute(block, "ctx", [(i - 4 * n, i) for i in range(4 * n, ctx)])

    trips = range(1, DEPTH + 1)
    kv0 = jnp.concatenate([keys, values], axis=0)
    k1, kv3, v1 = ring(keys, 1), ring(kv0, 3), ring(values, 1)

    def sinks_of(first, second):
        return jnp.concatenate([first[:SINK], second[:SINK]], axis=0)

    flat = [a.reshape(BLOCK * heads, LANES) for a in (query_states, output_grad)]
    query, grad = pick(at, flat, heads)
    leaving, _ = lax.optimization_barrier((query, k1))
    visitors = [down(leaving, n) for n in trips]
    k2, v2 = ring(k1, 1), ring(kv3[BLOCK:], -1)
    gate = jnp.sum(jnp.where(head_flags == 1, gate_values, 0.0))[None]

    full_rows = (DEPTH + 1) * BLOCK
    acc, ml = call(
        functools.partial(early_kernel, scale),
        [at],
        [query, *visitors, kv0, k1, v1, kv3],
        [shape(full_rows, f32)] * 2,
        [
            VMEM((full_rows, LANES), bf16),
            VMEM((3 * BLOCK, LANES), bf16),
            VMEM((3 * BLOCK, 2 * LANES), bf16),
        ],
        cost(12),
    )
    sinks = sinks_of(keys, values)
    for place, pair in ((1, (k1, v1)), (2, (k2, v2)), (3, (kv3[:BLOCK], kv3[BLOCK:]))):
        sinks = jnp.where(index == place, sinks_of(*pair), sinks)
    level = index // 4
    moved = [
        lax.ppermute(sinks, "ctx", [(i, i + 4 * n) for i in range(4)]) for n in trips
    ]
    for n, got in zip(trips, moved):
        sinks = jnp.where(level == n, got, sinks)
    own, lse, *parts = call(
        functools.partial(late_kernel, scale),
        [at],
        [query, *visitors, k2, v2, acc, ml],
        [shape(BLOCK, f32), shape(ROWS, f32)] + [shape(BLOCK + TAIL, bf16)] * DEPTH,
        [VMEM((BLOCK, 2 * LANES), bf16), VMEM((TAIL, LANES), f32)],
        cost(4),
    )
    parts = [home(part, n) for n, part in zip(trips, parts)]
    window = [kv0, k1, v1, k2, v2, sinks]
    scratch = [
        VMEM((3 * BLOCK, LANES), bf16),
        VMEM((3 * BLOCK, 2 * LANES), bf16),
        VMEM((LANES, LANES), bf16),
        VMEM((LANES, 2 * LANES), bf16),
    ]
    [near_one] = call(
        functools.partial(near_kernel, scale, 1, 256, 4, 0),
        [at],
        [query, *window],
        [shape(BLOCK, f32)],
        scratch,
        cost(2.5),
    )
    def near_half(queries, part):
        return call(
            functools.partial(near_kernel, scale, heads, 128, 2, part * (BLOCK // 2)),
            [at],
            [queries, *window],
            [shape(BLOCK // 2 * heads, bf16)],
            scratch,
            cost(4.5),
        )[0]

    first_half = near_half(flat[0], 0)
    norm = 1.0 / math.sqrt(lax.axis_size("dp") * BLOCK * ctx * LANES)
    devices = lax.axis_size("dp") * lax.axis_size("head") * ctx
    mixed, row = call(
        functools.partial(merge_kernel, norm),
        [at, gate],
        [own, lse, *parts, near_one, grad],
        [shape(BLOCK, bf16), shape(devices, f32)],
        [],
        cost(0.1),
    )
    everyone = lax.all_to_all(row, ("dp", "head", "ctx"), 0, 0, tiled=True)
    gate_grad = jnp.sum(everyone, axis=0)[: heads * lax.axis_size("head")]
    rest, _ = lax.optimization_barrier((flat[0], row))
    near_all = jnp.concatenate([first_half, near_half(rest, 1)], axis=0)
    near_all = near_all.reshape(1, BLOCK, heads, LANES)
    blended = jnp.where(marked[None], mixed[None, :, None, :], near_all)
    return (blended, gate_grad)


def solution(mesh):
    spec = P("dp", "ctx", "head", None)
    return jax.shard_map(
        on_device,
        mesh=mesh,
        in_specs=(spec, spec, spec, P("head"), P("head"), spec),
        out_specs=(spec, P()),
        check_vma=False,
    )
```

```python
import functools
import math

import jax
import jax.numpy as jnp
from jax import lax
from jax.experimental import pallas as pl
from jax.experimental.pallas import tpu as pltpu
from jax.sharding import PartitionSpec as P

SINK = 64
WINDOW = 2048
BLOCK = 1024
TILE = 512
UNROLL = 2
CHUNK = 512
ROWS = 8
TAIL = 32
DEPTH = 3
LANES = 128
VMEM = pltpu.VMEM
LOG2E = 1.4426950408889634
NEG = -1e30


def params():
    return pltpu.CompilerParams(vmem_limit_bytes=44 * 2**20)


def cost(units, bytes_accessed=4 * 2**20):
    return pl.CostEstimate(
        flops=int(units * 4 * BLOCK * BLOCK * LANES),
        bytes_accessed=bytes_accessed,
        transcendentals=int(units * BLOCK * BLOCK),
    )


def scores_of(q, k):
    return lax.dot_general(q, k, (((1,), (1,)), ((), ())), preferred_element_type=jnp.float32)


def one_pass(scores, values, scale, before=None):
    top = functools.reduce(
        jnp.maximum, [jnp.max(s, axis=1, keepdims=True) for s in scores]
    ) * scale
    if before is not None:
        top = jnp.maximum(top, before[0])
    update = functools.reduce(
        jnp.add,
        [
            jnp.dot(
                jnp.exp2(s * scale - top).astype(jnp.bfloat16),
                v(),
                preferred_element_type=jnp.float32,
            )
            for s, v in zip(scores, values)
        ],
    )
    total, acc = update[:, LANES:], update[:, :LANES]
    if before is not None:
        factor = jnp.exp2(before[0] - top)
        total = total + before[1] * factor
        acc = acc + before[2] * factor
    return top, total, acc


def take(ref, first, count):
    return ref[pl.ds(first, count), :]


def put_values(dest, first, source):
    rows = source.shape[0]
    dest[pl.ds(first, rows), 0:LANES] = source
    dest[pl.ds(first, rows), LANES : 2 * LANES] = jnp.ones((rows, LANES), jnp.bfloat16)


def pick_kernel(at, q, g, query_ref, grad_ref):
    rows, heads = query_ref.shape[0], q.shape[0] // query_ref.shape[0]
    row = lax.broadcasted_iota(jnp.int32, (rows, heads * rows), 0)
    col = lax.broadcasted_iota(jnp.int32, (rows, heads * rows), 1)
    chosen = jnp.where(col == heads * row + at[2], 1.0, 0.0).astype(jnp.bfloat16)
    for source, dest in ((q, query_ref), (g, grad_ref)):
        moved = jnp.dot(chosen, source[...], preferred_element_type=jnp.float32)
        dest[...] = moved.astype(jnp.bfloat16)


def pick(at, arrays, heads):
    rows = 2 * LANES
    return pl.pallas_call(
        pick_kernel,
        grid=(BLOCK // rows,),
        out_shape=[shape(BLOCK, jnp.bfloat16)] * 2,
        in_specs=[pl.BlockSpec(memory_space=pltpu.SMEM)]
        + [pl.BlockSpec((heads * rows, LANES), lambda n: (n, 0))] * 2,
        out_specs=[pl.BlockSpec((rows, LANES), lambda n: (n, 0))] * 2,
        compiler_params=params(),
        cost_estimate=cost(20),
    )(at, *arrays)


def early_kernel(scale, lead, at, qa, qb, kv0, k1, v1, kv3, acc_ref, ml_ref, qs, ks, vs):
    index = at[0]
    sets = 4 - index // 4
    for n, ref in enumerate((qa, qb)):
        qs[pl.ds(n * BLOCK, BLOCK), :] = ref[...]
    for n, ref in ((0, kv0), (2, kv3)):
        ks[pl.ds(n * BLOCK, BLOCK), :] = ref[0:BLOCK, :]
        put_values(vs, n * BLOCK, ref[BLOCK : 2 * BLOCK, :])
    ks[BLOCK : 2 * BLOCK, :] = k1[...]
    put_values(vs, BLOCK, v1[...])
    for n, least in ((1, 1), (2, 3)):

        @pl.when(index < least)
        def _():
            ks[n * BLOCK : (n + 1) * BLOCK, :] = kv0[0:BLOCK, :]
            vs[n * BLOCK : (n + 1) * BLOCK, :] = jnp.zeros((BLOCK, 2 * LANES), jnp.bfloat16)

    row = lax.broadcasted_iota(jnp.int32, (TILE, CHUNK), 0)
    col = lax.broadcasted_iota(jnp.int32, (TILE, CHUNK), 1)
    ahead = col - row
    lane = lax.broadcasted_iota(jnp.int32, (TILE, LANES), 1)

    def keep(rows, state):
        top, total, acc = state
        acc_ref[rows, :] = acc
        ml_ref[rows, :] = jnp.where(lane < LANES // 2, top, total)

    def fast(first, causal):
        rows = [pl.ds(pl.multiple_of(first + u * TILE, TILE), TILE) for u in range(UNROLL)]
        every = []
        for u in range(UNROLL):
            scores = []
            for c in range(0, 3 * BLOCK, CHUNK):
                s = scores_of(qs[rows[u], :], ks[c : c + CHUNK, :])
                if causal and c < BLOCK:
                    s = jnp.where(ahead <= u * TILE - c, s, NEG)
                elif causal:
                    s = jnp.where(index >= (1 if c < 2 * BLOCK else 3), s, NEG)
                scores.append(s)
            every.append(scores)
        values = [functools.partial(take, vs, c, CHUNK) for c in range(0, 3 * BLOCK, CHUNK)]
        for u in range(UNROLL):
            keep(rows[u], one_pass(every[u], values, scale))

    if lead == 0:
        fast(0, True)

    def step(t, _):
        fast(t * BLOCK, False)
        return 0

    lax.fori_loop(1 if lead == 0 else 0, jnp.clip(sets - lead, 0, 2), step, 0)


def late_kernel(scale, at, q0, q1, q2, q3, k2, v2, acc_a, ml_a, acc_b, ml_b, own_ref, lse_ref, p1, p2, p3, vs, tail):
    index = at[0]
    sets = 4 - index // 4
    put_values(vs, 0, v2[...])
    row = lax.broadcasted_iota(jnp.int32, (LANES, LANES), 0)
    diagonal = row == lax.broadcasted_iota(jnp.int32, (LANES, LANES), 1)
    groups = TILE // LANES

    def finish(u, state, dest):
        top, total, acc = state
        dest[u * TILE : (u + 1) * TILE, :] = (acc / total).astype(dest.dtype)
        lse = top + jnp.log2(total)
        for g in range(groups):
            part = jnp.where(diagonal, lse[g * LANES : (g + 1) * LANES, :], 0.0)
            spot = u * groups + g
            tail[spot : spot + 1, :] = jnp.sum(part, axis=0, keepdims=True)

    def before(number):
        acc, ml = (acc_a, ml_a) if number < 4 else (acc_b, ml_b)
        rows = slice(number % 4 * TILE, (number % 4 + 1) * TILE)
        ml = ml[rows, :]
        return ml[:, 0:1], ml[:, LANES // 2 : LANES // 2 + 1], acc[rows, :]

    for n, (query, dest) in enumerate(((q0, own_ref), (q1, p1), (q2, p2), (q3, p3))):

        @pl.when((index >= 2) & (n < sets))
        def _():
            every = [
                [
                    scores_of(query[u * TILE : (u + 1) * TILE, :], k2[c : c + CHUNK, :])
                    for c in range(0, BLOCK, CHUNK)
                ]
                for u in range(UNROLL)
            ]
            values = [functools.partial(take, vs, c, CHUNK) for c in range(0, BLOCK, CHUNK)]
            for u in range(UNROLL):
                finish(u, one_pass(every[u], values, scale, before(n * UNROLL + u)), dest)

        @pl.when((index < 2) & (n < sets))
        def _():
            for u in range(UNROLL):
                top, total, acc = before(n * UNROLL + u)
                finish(u, (top, jnp.broadcast_to(total, acc.shape), acc), dest)

        @pl.when(n < sets)
        def _():
            if n == 0:
                lse_ref[...] = tail[...]
            else:
                value = tail[...]
                high = value.astype(jnp.bfloat16).astype(jnp.float32)
                middle = (value - high).astype(jnp.bfloat16).astype(jnp.float32)
                low = value - high - middle
                dest[BLOCK : BLOCK + TAIL, :] = jnp.concatenate(
                    [high, middle, low, jnp.zeros_like(low)], axis=0
                ).astype(jnp.bfloat16)

        @pl.when(n >= sets)
        def _():
            dest[...] = jnp.zeros_like(dest)


def near_kernel(scale, per_pos, positions, unroll, start, at, q, kv0, k1, v1, k2, v2, sinks, out_ref, ks, vs, fk, fv):
    index = at[0]
    ks[0:BLOCK, :] = k2[...]
    put_values(vs, 0, v2[...])
    ks[BLOCK : 2 * BLOCK, :] = k1[...]
    put_values(vs, BLOCK, v1[...])
    ks[2 * BLOCK : 3 * BLOCK, :] = kv0[0:BLOCK, :]
    put_values(vs, 2 * BLOCK, kv0[BLOCK : 2 * BLOCK, :])
    blank = jnp.zeros((LANES - SINK, LANES), jnp.bfloat16)
    fk[0:SINK, :] = sinks[0:SINK, :]
    fk[SINK:LANES, :] = blank
    put_values(fv, 0, sinks[SINK : 2 * SINK, :])
    put_values(fv, SINK, blank)
    tile = positions * per_pos
    width = WINDOW + positions
    row = lax.broadcasted_iota(jnp.int32, (tile, positions), 0) // per_pos
    col = lax.broadcasted_iota(jnp.int32, (tile, positions), 1)
    sink_row = lax.broadcasted_iota(jnp.int32, (tile, LANES), 0) // per_pos
    sink_col = lax.broadcasted_iota(jnp.int32, (tile, LANES), 1)
    first = (2 - index) * BLOCK
    cuts = [0, *range(positions, WINDOW, CHUNK), WINDOW, width]

    def group(t, partial_window):
        every, rows, begins = [], [], []
        for u in range(unroll):
            number = t * unroll + u
            rows.append(pl.ds(pl.multiple_of(number * tile, tile), tile))
            begin = pl.multiple_of(start + number * positions, positions)
            begins.append(begin)
            query = q[pl.ds(pl.multiple_of((start + number * positions) * per_pos, tile), tile), :]
            scores = []
            for low, high in zip(cuts, cuts[1:]):
                s = scores_of(query, ks[pl.ds(pl.multiple_of(begin + low, LANES), high - low), :])
                if partial_window:
                    column = lax.broadcasted_iota(jnp.int32, (1, high - low), 1) + begin + low
                    s = s + jnp.where(column >= first, 0.0, NEG)
                if low == 0:
                    s = jnp.where(col > row, s, NEG)
                if low == WINDOW:
                    s = jnp.where(col <= row, s, NEG)
                scores.append(s)
            far = scores_of(query, fk[...])
            reach = index * BLOCK + begin + sink_row - sink_col
            scores.append(jnp.where((sink_col < SINK) & (reach >= WINDOW), far, NEG))
            every.append(scores)
        for u in range(unroll):
            values = [
                functools.partial(take, vs, pl.multiple_of(begins[u] + low, LANES), high - low)
                for low, high in zip(cuts, cuts[1:])
            ]
            _, total, acc = one_pass(every[u], values + [functools.partial(take, fv, 0, LANES)], scale)
            out_ref[rows[u], :] = (acc / total).astype(out_ref.dtype)

    for cond, partial_window in ((index >= 2, False), (index < 2, True)):

        @pl.when(cond)
        def _():
            def step(t, _):
                group(t, partial_window)
                return 0

            lax.fori_loop(0, out_ref.shape[0] // (tile * unroll), step, 0)


def merge_kernel(norm, at, gate, own, lse, p1, p2, p3, near, grad, mix_ref, row_ref):
    level = at[0] // 4
    gated = gate[0]
    logs = [lse[...]]
    for n, ref in ((1, p1), (2, p2), (3, p3)):
        tail = ref[BLOCK : BLOCK + TAIL, :].astype(jnp.float32)
        value = tail[0:ROWS] + tail[ROWS : 2 * ROWS] + tail[2 * ROWS : 3 * ROWS]
        logs.append(jnp.where(level >= n, value, NEG))
    top = functools.reduce(jnp.maximum, logs)
    shares = [jnp.exp2(x - top) for x in logs]
    whole = functools.reduce(jnp.add, shares)
    shares = [x / whole for x in shares]
    total = jnp.zeros((1, LANES), jnp.float32)
    for g in range(BLOCK // LANES):
        rows = slice(g * LANES, (g + 1) * LANES)
        columns = [jnp.broadcast_to(x[g : g + 1, :], (LANES, LANES)).T for x in shares]
        full = columns[0] * own[rows, :]
        for column, ref in zip(columns[1:], (p1, p2, p3)):
            full = full + column * ref[rows, :].astype(jnp.float32)
        close = near[rows, :]
        mix_ref[rows, :] = (gated * full + (1.0 - gated) * close).astype(jnp.bfloat16)
        total = total + jnp.sum(
            grad[rows, :].astype(jnp.float32) * (full - close), axis=0, keepdims=True
        )
    value = jnp.sum(total, axis=1, keepdims=True) * norm
    lane = lax.broadcasted_iota(jnp.int32, row_ref.shape, 1)
    row_ref[...] = jnp.where(lane == at[1], value, 0.0)


def call(kernel, scalars, arrays, outs, scratch, estimate):
    specs = [pl.BlockSpec(memory_space=pltpu.SMEM)] * len(scalars)
    specs += [pl.BlockSpec(memory_space=VMEM)] * len(arrays)
    return pl.pallas_call(
        kernel,
        out_shape=outs,
        in_specs=specs,
        out_specs=[pl.BlockSpec(memory_space=VMEM)] * len(outs),
        scratch_shapes=scratch,
        compiler_params=params(),
        cost_estimate=estimate,
    )(*scalars, *arrays)


def shape(rows, dtype):
    return jax.ShapeDtypeStruct((rows, LANES), dtype)


def on_device(query_states, key_states, value_states, gate_values, head_flags, output_grad):
    bf16, f32 = jnp.bfloat16, jnp.float32
    heads = head_flags.shape[0]
    ctx = lax.axis_size("ctx")
    index = lax.axis_index("ctx")
    scale = LOG2E / math.sqrt(LANES)
    keys = key_states.reshape(BLOCK, LANES)
    values = value_states.reshape(BLOCK, LANES)
    marked = (head_flags == 1)[None, :, None]
    which = jnp.sum(head_flags * jnp.arange(heads, dtype=jnp.int32))

    at = jnp.stack([index, lax.axis_index("head") * heads + which, which]).astype(jnp.int32)

    def ring(block, shift):
        return lax.ppermute(block, "ctx", [(i, (i + shift) % ctx) for i in range(ctx)])

    def down(block, n):
        return lax.ppermute(block, "ctx", [(i, i - 4 * n) for i in range(4 * n, ctx)])

    def home(block, n):
        return lax.ppermute(block, "ctx", [(i - 4 * n, i) for i in range(4 * n, ctx)])

    trips = range(1, DEPTH + 1)
    kv0 = jnp.concatenate([keys, values], axis=0)
    k1, kv3, v1 = ring(keys, 1), ring(kv0, 3), ring(values, 1)

    def sinks_of(first, second):
        return jnp.concatenate([first[:SINK], second[:SINK]], axis=0)

    flat = [a.reshape(BLOCK * heads, LANES) for a in (query_states, output_grad)]
    query, grad = pick(at, flat, heads)
    leaving, _ = lax.optimization_barrier((query, k1))
    visitors = [down(leaving, n) for n in trips]
    k2, v2 = ring(k1, 1), ring(kv3[BLOCK:], -1)
    gate = jnp.sum(jnp.where(head_flags == 1, gate_values, 0.0))[None]

    def early(lead, first, second):
        return call(
            functools.partial(early_kernel, scale, lead),
            [at],
            [first, second, kv0, k1, v1, kv3],
            [shape(2 * BLOCK, f32)] * 2,
            [
                VMEM((2 * BLOCK, LANES), bf16),
                VMEM((3 * BLOCK, LANES), bf16),
                VMEM((3 * BLOCK, 2 * LANES), bf16),
            ],
            cost(6),
        )

    early_states = early(0, query, visitors[0])
    early_states = [*early_states, *early(2, visitors[1], visitors[2])]
    sinks = sinks_of(keys, values)
    for place, pair in ((1, (k1, v1)), (2, (k2, v2)), (3, (kv3[:BLOCK], kv3[BLOCK:]))):
        sinks = jnp.where(index == place, sinks_of(*pair), sinks)
    level = index // 4
    moved = [
        lax.ppermute(sinks, "ctx", [(i, i + 4 * n) for i in range(4)]) for n in trips
    ]
    for n, got in zip(trips, moved):
        sinks = jnp.where(level == n, got, sinks)
    own, lse, *parts = call(
        functools.partial(late_kernel, scale),
        [at],
        [query, *visitors, k2, v2, *early_states],
        [shape(BLOCK, f32), shape(ROWS, f32)] + [shape(BLOCK + TAIL, bf16)] * DEPTH,
        [VMEM((BLOCK, 2 * LANES), bf16), VMEM((ROWS, LANES), f32)],
        cost(4),
    )
    parts = [home(part, n) for n, part in zip(trips, parts)]
    window = [kv0, k1, v1, k2, v2, sinks]
    scratch = [
        VMEM((3 * BLOCK, LANES), bf16),
        VMEM((3 * BLOCK, 2 * LANES), bf16),
        VMEM((LANES, LANES), bf16),
        VMEM((LANES, 2 * LANES), bf16),
    ]
    [near_one] = call(
        functools.partial(near_kernel, scale, 1, 256, 4, 0),
        [at],
        [query, *window],
        [shape(BLOCK, f32)],
        scratch,
        cost(2.5),
    )
    def near_half(queries, part):
        return call(
            functools.partial(near_kernel, scale, heads, 128, 2, part * (BLOCK // 2)),
            [at],
            [queries, *window],
            [shape(BLOCK // 2 * heads, bf16)],
            scratch,
            cost(4.5),
        )[0]

    first_half = near_half(flat[0], 0)
    norm = 1.0 / math.sqrt(lax.axis_size("dp") * BLOCK * ctx * LANES)
    devices = lax.axis_size("dp") * lax.axis_size("head") * ctx
    mixed, row = call(
        functools.partial(merge_kernel, norm),
        [at, gate],
        [own, lse, *parts, near_one, grad],
        [shape(BLOCK, bf16), shape(devices, f32)],
        [],
        cost(0.1),
    )
    everyone = lax.all_to_all(row, ("dp", "head", "ctx"), 0, 0, tiled=True)
    gate_grad = jnp.sum(everyone, axis=0)[: heads * lax.axis_size("head")]
    rest, _ = lax.optimization_barrier((flat[0], row))
    near_all = jnp.concatenate([first_half, near_half(rest, 1)], axis=0)
    near_all = near_all.reshape(1, BLOCK, heads, LANES)
    blended = jnp.where(marked[None], mixed[None, :, None, :], near_all)
    return (blended, gate_grad)


def solution(mesh):
    spec = P("dp", "ctx", "head", None)
    return jax.shard_map(
        on_device,
        mesh=mesh,
        in_specs=(spec, spec, spec, P("head"), P("head"), spec),
        out_specs=(spec, P()),
        check_vma=False,
    )
```

```python
import functools
import math

import jax
import jax.numpy as jnp
from jax import lax
from jax.experimental import pallas as pl
from jax.experimental.pallas import tpu as pltpu
from jax.sharding import PartitionSpec as P

SINK = 64
WINDOW = 2048
BLOCK = 1024
TILE = 512
UNROLL = 2
CHUNK = 512
ROWS = 8
TAIL = 32
DEPTH = 3
LANES = 128
VMEM = pltpu.VMEM
LOG2E = 1.4426950408889634
NEG = -1e30


def params():
    return pltpu.CompilerParams(vmem_limit_bytes=44 * 2**20)


def cost(units, bytes_accessed=4 * 2**20):
    return pl.CostEstimate(
        flops=int(units * 4 * BLOCK * BLOCK * LANES),
        bytes_accessed=bytes_accessed,
        transcendentals=int(units * BLOCK * BLOCK),
    )


def scores_of(q, k):
    return lax.dot_general(q, k, (((1,), (1,)), ((), ())), preferred_element_type=jnp.float32)


def one_pass(scores, values, scale, before=None):
    top = functools.reduce(
        jnp.maximum, [jnp.max(s, axis=1, keepdims=True) for s in scores]
    ) * scale
    if before is not None:
        top = jnp.maximum(top, before[0])
    update = functools.reduce(
        jnp.add,
        [
            jnp.dot(
                jnp.exp2(s * scale - top).astype(jnp.bfloat16),
                v(),
                preferred_element_type=jnp.float32,
            )
            for s, v in zip(scores, values)
        ],
    )
    total, acc = update[:, LANES:], update[:, :LANES]
    if before is not None:
        factor = jnp.exp2(before[0] - top)
        total = total + before[1] * factor
        acc = acc + before[2] * factor
    return top, total, acc


def take(ref, first, count):
    return ref[pl.ds(first, count), :]


def put_values(dest, first, source):
    rows = source.shape[0]
    dest[pl.ds(first, rows), 0:LANES] = source
    dest[pl.ds(first, rows), LANES : 2 * LANES] = jnp.ones((rows, LANES), jnp.bfloat16)


def pick_kernel(at, q, g, query_ref, grad_ref):
    rows, heads = query_ref.shape[0], q.shape[0] // query_ref.shape[0]
    row = lax.broadcasted_iota(jnp.int32, (rows, heads * rows), 0)
    col = lax.broadcasted_iota(jnp.int32, (rows, heads * rows), 1)
    chosen = jnp.where(col == heads * row + at[2], 1.0, 0.0).astype(jnp.bfloat16)
    for source, dest in ((q, query_ref), (g, grad_ref)):
        moved = jnp.dot(chosen, source[...], preferred_element_type=jnp.float32)
        dest[...] = moved.astype(jnp.bfloat16)


def pick(at, arrays, heads):
    rows = 2 * LANES
    return pl.pallas_call(
        pick_kernel,
        grid=(BLOCK // rows,),
        out_shape=[shape(BLOCK, jnp.bfloat16)] * 2,
        in_specs=[pl.BlockSpec(memory_space=pltpu.SMEM)]
        + [pl.BlockSpec((heads * rows, LANES), lambda n: (n, 0))] * 2,
        out_specs=[pl.BlockSpec((rows, LANES), lambda n: (n, 0))] * 2,
        compiler_params=params(),
        cost_estimate=cost(20),
    )(at, *arrays)


def early_kernel(scale, lead, at, qa, qb, kv0, k1, v1, kv3, acc_ref, ml_ref, qs, ks, vs):
    index = at[0]
    sets = 4 - index // 4
    for n, ref in enumerate((qa, qb)):
        qs[pl.ds(n * BLOCK, BLOCK), :] = ref[...]
    for n, ref in ((0, kv0), (2, kv3)):
        ks[pl.ds(n * BLOCK, BLOCK), :] = ref[0:BLOCK, :]
        put_values(vs, n * BLOCK, ref[BLOCK : 2 * BLOCK, :])
    ks[BLOCK : 2 * BLOCK, :] = k1[...]
    put_values(vs, BLOCK, v1[...])
    for n, least in ((1, 1), (2, 3)):

        @pl.when(index < least)
        def _():
            ks[n * BLOCK : (n + 1) * BLOCK, :] = kv0[0:BLOCK, :]
            vs[n * BLOCK : (n + 1) * BLOCK, :] = jnp.zeros((BLOCK, 2 * LANES), jnp.bfloat16)

    row = lax.broadcasted_iota(jnp.int32, (TILE, CHUNK), 0)
    col = lax.broadcasted_iota(jnp.int32, (TILE, CHUNK), 1)
    ahead = col - row
    lane = lax.broadcasted_iota(jnp.int32, (TILE, LANES), 1)

    def keep(rows, state):
        top, total, acc = state
        acc_ref[rows, :] = acc
        ml_ref[rows, :] = jnp.where(lane < LANES // 2, top, total)

    def fast(first, causal):
        rows = [pl.ds(pl.multiple_of(first + u * TILE, TILE), TILE) for u in range(UNROLL)]
        every = []
        for u in range(UNROLL):
            scores = []
            for c in range(0, 3 * BLOCK, CHUNK):
                s = scores_of(qs[rows[u], :], ks[c : c + CHUNK, :])
                if causal and c < BLOCK:
                    s = jnp.where(ahead <= u * TILE - c, s, NEG)
                elif causal:
                    s = jnp.where(index >= (1 if c < 2 * BLOCK else 3), s, NEG)
                scores.append(s)
            every.append(scores)
        values = [functools.partial(take, vs, c, CHUNK) for c in range(0, 3 * BLOCK, CHUNK)]
        for u in range(UNROLL):
            keep(rows[u], one_pass(every[u], values, scale))

    if lead == 0:
        fast(0, True)

    def step(t, _):
        fast(t * BLOCK, False)
        return 0

    lax.fori_loop(1 if lead == 0 else 0, jnp.clip(sets - lead, 0, 2), step, 0)


def late_kernel(scale, first, at, *refs):
    if first == 0:
        q0, k2, v2, acc_a, ml_a, own_ref, lse_ref, vs, tail = refs
        jobs = [(0, q0, own_ref)]
    else:
        q1, q2, q3, k2, v2, acc_a, ml_a, acc_b, ml_b, p1, p2, p3, vs, tail = refs
        jobs = [(1, q1, p1), (2, q2, p2), (3, q3, p3)]
    index = at[0]
    sets = 4 - index // 4
    put_values(vs, 0, v2[...])
    row = lax.broadcasted_iota(jnp.int32, (LANES, LANES), 0)
    diagonal = row == lax.broadcasted_iota(jnp.int32, (LANES, LANES), 1)
    groups = TILE // LANES

    def finish(u, state, dest):
        top, total, acc = state
        dest[u * TILE : (u + 1) * TILE, :] = (acc / total).astype(dest.dtype)
        lse = top + jnp.log2(total)
        for g in range(groups):
            part = jnp.where(diagonal, lse[g * LANES : (g + 1) * LANES, :], 0.0)
            spot = u * groups + g
            tail[spot : spot + 1, :] = jnp.sum(part, axis=0, keepdims=True)

    def before(number):
        acc, ml = (acc_a, ml_a) if number < 4 else (acc_b, ml_b)
        rows = slice(number % 4 * TILE, (number % 4 + 1) * TILE)
        ml = ml[rows, :]
        return ml[:, 0:1], ml[:, LANES // 2 : LANES // 2 + 1], acc[rows, :]

    for n, query, dest in jobs:

        @pl.when((index >= 2) & (n < sets))
        def _():
            every = [
                [
                    scores_of(query[u * TILE : (u + 1) * TILE, :], k2[c : c + CHUNK, :])
                    for c in range(0, BLOCK, CHUNK)
                ]
                for u in range(UNROLL)
            ]
            values = [functools.partial(take, vs, c, CHUNK) for c in range(0, BLOCK, CHUNK)]
            for u in range(UNROLL):
                finish(u, one_pass(every[u], values, scale, before(n * UNROLL + u)), dest)

        @pl.when((index < 2) & (n < sets))
        def _():
            for u in range(UNROLL):
                top, total, acc = before(n * UNROLL + u)
                finish(u, (top, jnp.broadcast_to(total, acc.shape), acc), dest)

        @pl.when(n < sets)
        def _():
            if n == 0:
                lse_ref[...] = tail[...]
            else:
                value = tail[...]
                high = value.astype(jnp.bfloat16).astype(jnp.float32)
                middle = (value - high).astype(jnp.bfloat16).astype(jnp.float32)
                low = value - high - middle
                dest[BLOCK : BLOCK + TAIL, :] = jnp.concatenate(
                    [high, middle, low, jnp.zeros_like(low)], axis=0
                ).astype(jnp.bfloat16)

        @pl.when(n >= sets)
        def _():
            dest[...] = jnp.zeros_like(dest)


def near_kernel(scale, per_pos, positions, unroll, start, at, q, kv0, k1, v1, k2, v2, sinks, out_ref, ks, vs, fk, fv):
    index = at[0]
    ks[0:BLOCK, :] = k2[...]
    put_values(vs, 0, v2[...])
    ks[BLOCK : 2 * BLOCK, :] = k1[...]
    put_values(vs, BLOCK, v1[...])
    ks[2 * BLOCK : 3 * BLOCK, :] = kv0[0:BLOCK, :]
    put_values(vs, 2 * BLOCK, kv0[BLOCK : 2 * BLOCK, :])
    blank = jnp.zeros((LANES - SINK, LANES), jnp.bfloat16)
    fk[0:SINK, :] = sinks[0:SINK, :]
    fk[SINK:LANES, :] = blank
    put_values(fv, 0, sinks[SINK : 2 * SINK, :])
    put_values(fv, SINK, blank)
    tile = positions * per_pos
    width = WINDOW + positions
    row = lax.broadcasted_iota(jnp.int32, (tile, positions), 0) // per_pos
    col = lax.broadcasted_iota(jnp.int32, (tile, positions), 1)
    sink_row = lax.broadcasted_iota(jnp.int32, (tile, LANES), 0) // per_pos
    sink_col = lax.broadcasted_iota(jnp.int32, (tile, LANES), 1)
    first = (2 - index) * BLOCK
    cuts = [0, *range(positions, WINDOW, CHUNK), WINDOW, width]

    def group(t, partial_window):
        every, rows, begins = [], [], []
        for u in range(unroll):
            number = t * unroll + u
            rows.append(pl.ds(pl.multiple_of(number * tile, tile), tile))
            begin = pl.multiple_of(start + number * positions, positions)
            begins.append(begin)
            query = q[pl.ds(pl.multiple_of((start + number * positions) * per_pos, tile), tile), :]
            scores = []
            for low, high in zip(cuts, cuts[1:]):
                s = scores_of(query, ks[pl.ds(pl.multiple_of(begin + low, LANES), high - low), :])
                if partial_window:
                    column = lax.broadcasted_iota(jnp.int32, (1, high - low), 1) + begin + low
                    s = s + jnp.where(column >= first, 0.0, NEG)
                if low == 0:
                    s = jnp.where(col > row, s, NEG)
                if low == WINDOW:
                    s = jnp.where(col <= row, s, NEG)
                scores.append(s)
            far = scores_of(query, fk[...])
            reach = index * BLOCK + begin + sink_row - sink_col
            scores.append(jnp.where((sink_col < SINK) & (reach >= WINDOW), far, NEG))
            every.append(scores)
        for u in range(unroll):
            values = [
                functools.partial(take, vs, pl.multiple_of(begins[u] + low, LANES), high - low)
                for low, high in zip(cuts, cuts[1:])
            ]
            _, total, acc = one_pass(every[u], values + [functools.partial(take, fv, 0, LANES)], scale)
            out_ref[rows[u], :] = (acc / total).astype(out_ref.dtype)

    for cond, partial_window in ((index >= 2, False), (index < 2, True)):

        @pl.when(cond)
        def _():
            def step(t, _):
                group(t, partial_window)
                return 0

            lax.fori_loop(0, out_ref.shape[0] // (tile * unroll), step, 0)


def merge_kernel(norm, at, gate, own, lse, p1, p2, p3, near, grad, mix_ref, row_ref):
    level = at[0] // 4
    gated = gate[0]
    logs = [lse[...]]
    for n, ref in ((1, p1), (2, p2), (3, p3)):
        tail = ref[BLOCK : BLOCK + TAIL, :].astype(jnp.float32)
        value = tail[0:ROWS] + tail[ROWS : 2 * ROWS] + tail[2 * ROWS : 3 * ROWS]
        logs.append(jnp.where(level >= n, value, NEG))
    top = functools.reduce(jnp.maximum, logs)
    shares = [jnp.exp2(x - top) for x in logs]
    whole = functools.reduce(jnp.add, shares)
    shares = [x / whole for x in shares]
    total = jnp.zeros((1, LANES), jnp.float32)
    for g in range(BLOCK // LANES):
        rows = slice(g * LANES, (g + 1) * LANES)
        columns = [jnp.broadcast_to(x[g : g + 1, :], (LANES, LANES)).T for x in shares]
        full = columns[0] * own[rows, :]
        for column, ref in zip(columns[1:], (p1, p2, p3)):
            full = full + column * ref[rows, :].astype(jnp.float32)
        close = near[rows, :]
        mix_ref[rows, :] = (gated * full + (1.0 - gated) * close).astype(jnp.bfloat16)
        total = total + jnp.sum(
            grad[rows, :].astype(jnp.float32) * (full - close), axis=0, keepdims=True
        )
    value = jnp.sum(total, axis=1, keepdims=True) * norm
    lane = lax.broadcasted_iota(jnp.int32, row_ref.shape, 1)
    row_ref[...] = jnp.where(lane == at[1], value, 0.0)


def call(kernel, scalars, arrays, outs, scratch, estimate):
    specs = [pl.BlockSpec(memory_space=pltpu.SMEM)] * len(scalars)
    specs += [pl.BlockSpec(memory_space=VMEM)] * len(arrays)
    return pl.pallas_call(
        kernel,
        out_shape=outs,
        in_specs=specs,
        out_specs=[pl.BlockSpec(memory_space=VMEM)] * len(outs),
        scratch_shapes=scratch,
        compiler_params=params(),
        cost_estimate=estimate,
    )(*scalars, *arrays)


def shape(rows, dtype):
    return jax.ShapeDtypeStruct((rows, LANES), dtype)


def on_device(query_states, key_states, value_states, gate_values, head_flags, output_grad):
    bf16, f32 = jnp.bfloat16, jnp.float32
    heads = head_flags.shape[0]
    ctx = lax.axis_size("ctx")
    index = lax.axis_index("ctx")
    scale = LOG2E / math.sqrt(LANES)
    keys = key_states.reshape(BLOCK, LANES)
    values = value_states.reshape(BLOCK, LANES)
    marked = (head_flags == 1)[None, :, None]
    which = jnp.sum(head_flags * jnp.arange(heads, dtype=jnp.int32))

    at = jnp.stack([index, lax.axis_index("head") * heads + which, which]).astype(jnp.int32)

    def ring(block, shift):
        return lax.ppermute(block, "ctx", [(i, (i + shift) % ctx) for i in range(ctx)])

    def down(block, n):
        return lax.ppermute(block, "ctx", [(i, i - 4 * n) for i in range(4 * n, ctx)])

    def home(block, n):
        return lax.ppermute(block, "ctx", [(i - 4 * n, i) for i in range(4 * n, ctx)])

    trips = range(1, DEPTH + 1)
    kv0 = jnp.concatenate([keys, values], axis=0)
    k1, kv3, v1 = ring(keys, 1), ring(kv0, 3), ring(values, 1)

    def sinks_of(first, second):
        return jnp.concatenate([first[:SINK], second[:SINK]], axis=0)

    flat = [a.reshape(BLOCK * heads, LANES) for a in (query_states, output_grad)]
    query, grad = pick(at, flat, heads)
    leaving, _ = lax.optimization_barrier((query, k1))
    visitors = [down(leaving, n) for n in trips]
    k2, v2 = ring(k1, 1), ring(kv3[BLOCK:], -1)
    gate = jnp.sum(jnp.where(head_flags == 1, gate_values, 0.0))[None]

    def early(lead, first, second):
        return call(
            functools.partial(early_kernel, scale, lead),
            [at],
            [first, second, kv0, k1, v1, kv3],
            [shape(2 * BLOCK, f32)] * 2,
            [
                VMEM((2 * BLOCK, LANES), bf16),
                VMEM((3 * BLOCK, LANES), bf16),
                VMEM((3 * BLOCK, 2 * LANES), bf16),
            ],
            cost(6),
        )

    early_states = early(0, query, visitors[0])
    early_states = [*early_states, *early(2, visitors[1], visitors[2])]
    sinks = sinks_of(keys, values)
    for place, pair in ((1, (k1, v1)), (2, (k2, v2)), (3, (kv3[:BLOCK], kv3[BLOCK:]))):
        sinks = jnp.where(index == place, sinks_of(*pair), sinks)
    level = index // 4
    moved = [
        lax.ppermute(sinks, "ctx", [(i, i + 4 * n) for i in range(4)]) for n in trips
    ]
    for n, got in zip(trips, moved):
        sinks = jnp.where(level == n, got, sinks)
    late_scratch = [VMEM((BLOCK, 2 * LANES), bf16), VMEM((ROWS, LANES), f32)]
    parts = call(
        functools.partial(late_kernel, scale, 1),
        [at],
        [*visitors, k2, v2, *early_states],
        [shape(BLOCK + TAIL, bf16)] * DEPTH,
        late_scratch,
        cost(3),
    )
    own_k2, _ = lax.optimization_barrier((k2, sinks))
    own, lse = call(
        functools.partial(late_kernel, scale, 0),
        [at],
        [query, own_k2, v2, *early_states[:2]],
        [shape(BLOCK, f32), shape(ROWS, f32)],
        late_scratch,
        cost(1),
    )
    parts = [home(part, n) for n, part in zip(trips, parts)]
    window = [kv0, k1, v1, k2, v2]
    scratch = [
        VMEM((3 * BLOCK, LANES), bf16),
        VMEM((3 * BLOCK, 2 * LANES), bf16),
        VMEM((LANES, LANES), bf16),
        VMEM((LANES, 2 * LANES), bf16),
    ]
    [near_one] = call(
        functools.partial(near_kernel, scale, 1, 256, 4, 0),
        [at],
        [query, *window, sinks],
        [shape(BLOCK, f32)],
        scratch,
        cost(2.5),
    )
    def near_part(start, count, sink_rows):
        return call(
            functools.partial(near_kernel, scale, heads, 128, 2, start),
            [at],
            [flat[0], *window, sink_rows],
            [shape(count * heads, bf16)],
            scratch,
            cost(9 * count / BLOCK),
        )[0]

    ahead = BLOCK // 4
    first_part = near_part(0, ahead, sinks)
    norm = 1.0 / math.sqrt(lax.axis_size("dp") * BLOCK * ctx * LANES)
    devices = lax.axis_size("dp") * lax.axis_size("head") * ctx
    mixed, row = call(
        functools.partial(merge_kernel, norm),
        [at, gate],
        [own, lse, *parts, near_one, grad],
        [shape(BLOCK, bf16), shape(devices, f32)],
        [],
        cost(0.1),
    )
    everyone = lax.all_to_all(row, ("dp", "head", "ctx"), 0, 0, tiled=True)
    gate_grad = jnp.sum(everyone, axis=0)[: heads * lax.axis_size("head")]
    later, _ = lax.optimization_barrier((sinks, row))
    near_all = jnp.concatenate([first_part, near_part(ahead, BLOCK - ahead, later)], axis=0)
    near_all = near_all.reshape(1, BLOCK, heads, LANES)
    blended = jnp.where(marked[None], mixed[None, :, None, :], near_all)
    return (blended, gate_grad)


def solution(mesh):
    spec = P("dp", "ctx", "head", None)
    return jax.shard_map(
        on_device,
        mesh=mesh,
        in_specs=(spec, spec, spec, P("head"), P("head"), spec),
        out_specs=(spec, P()),
        check_vma=False,
    )
```

```python
import functools
import math

import jax
import jax.numpy as jnp
from jax import lax
from jax.experimental import pallas as pl
from jax.experimental.pallas import tpu as pltpu
from jax.sharding import PartitionSpec as P

SINK = 64
WINDOW = 2048
BLOCK = 1024
TILE = 512
UNROLL = 2
CHUNK = 512
ROWS = 8
TAIL = 32
DEPTH = 3
LANES = 128
VMEM = pltpu.VMEM
LOG2E = 1.4426950408889634
NEG = -1e30


def params():
    return pltpu.CompilerParams(vmem_limit_bytes=44 * 2**20)


def cost(units, bytes_accessed=4 * 2**20):
    return pl.CostEstimate(
        flops=int(units * 4 * BLOCK * BLOCK * LANES),
        bytes_accessed=bytes_accessed,
        transcendentals=int(units * BLOCK * BLOCK),
    )


def scores_of(q, k):
    return lax.dot_general(q, k, (((1,), (1,)), ((), ())), preferred_element_type=jnp.float32)


def one_pass(scores, values, scale, before=None):
    top = functools.reduce(
        jnp.maximum, [jnp.max(s, axis=1, keepdims=True) for s in scores]
    ) * scale
    if before is not None:
        top = jnp.maximum(top, before[0])
    update = functools.reduce(
        jnp.add,
        [
            jnp.dot(
                jnp.exp2(s * scale - top).astype(jnp.bfloat16),
                v(),
                preferred_element_type=jnp.float32,
            )
            for s, v in zip(scores, values)
        ],
    )
    total, acc = update[:, LANES:], update[:, :LANES]
    if before is not None:
        factor = jnp.exp2(before[0] - top)
        total = total + before[1] * factor
        acc = acc + before[2] * factor
    return top, total, acc


def take(ref, first, count):
    return ref[pl.ds(first, count), :]


def put_values(dest, first, source):
    rows = source.shape[0]
    dest[pl.ds(first, rows), 0:LANES] = source
    dest[pl.ds(first, rows), LANES : 2 * LANES] = jnp.ones((rows, LANES), jnp.bfloat16)


def pick_kernel(at, q, g, query_ref, grad_ref):
    rows, heads = query_ref.shape[0], q.shape[0] // query_ref.shape[0]
    row = lax.broadcasted_iota(jnp.int32, (rows, heads * rows), 0)
    col = lax.broadcasted_iota(jnp.int32, (rows, heads * rows), 1)
    chosen = jnp.where(col == heads * row + at[2], 1.0, 0.0).astype(jnp.bfloat16)
    for source, dest in ((q, query_ref), (g, grad_ref)):
        moved = jnp.dot(chosen, source[...], preferred_element_type=jnp.float32)
        dest[...] = moved.astype(jnp.bfloat16)


def pick(at, arrays, heads):
    rows = 2 * LANES
    return pl.pallas_call(
        pick_kernel,
        grid=(BLOCK // rows,),
        out_shape=[shape(BLOCK, jnp.bfloat16)] * 2,
        in_specs=[pl.BlockSpec(memory_space=pltpu.SMEM)]
        + [pl.BlockSpec((heads * rows, LANES), lambda n: (n, 0))] * 2,
        out_specs=[pl.BlockSpec((rows, LANES), lambda n: (n, 0))] * 2,
        compiler_params=params(),
        cost_estimate=cost(20),
    )(at, *arrays)


def early_kernel(scale, lead, at, qa, qb, kv0, k1, v1, kv3, acc_ref, ml_ref, qs, ks, vs):
    index = at[0]
    sets = 4 - index // 4
    for n, ref in enumerate((qa, qb)):
        qs[pl.ds(n * BLOCK, BLOCK), :] = ref[...]
    for n, ref in ((0, kv0), (2, kv3)):
        ks[pl.ds(n * BLOCK, BLOCK), :] = ref[0:BLOCK, :]
        put_values(vs, n * BLOCK, ref[BLOCK : 2 * BLOCK, :])
    ks[BLOCK : 2 * BLOCK, :] = k1[...]
    put_values(vs, BLOCK, v1[...])
    for n, least in ((1, 1), (2, 3)):

        @pl.when(index < least)
        def _():
            ks[n * BLOCK : (n + 1) * BLOCK, :] = kv0[0:BLOCK, :]
            vs[n * BLOCK : (n + 1) * BLOCK, :] = jnp.zeros((BLOCK, 2 * LANES), jnp.bfloat16)

    row = lax.broadcasted_iota(jnp.int32, (TILE, CHUNK), 0)
    col = lax.broadcasted_iota(jnp.int32, (TILE, CHUNK), 1)
    ahead = col - row
    lane = lax.broadcasted_iota(jnp.int32, (TILE, LANES), 1)

    def keep(rows, state):
        top, total, acc = state
        acc_ref[rows, :] = acc
        ml_ref[rows, :] = jnp.where(lane < LANES // 2, top, total)

    def fast(first, causal):
        rows = [pl.ds(pl.multiple_of(first + u * TILE, TILE), TILE) for u in range(UNROLL)]
        every = []
        for u in range(UNROLL):
            scores = []
            for c in range(0, 3 * BLOCK, CHUNK):
                s = scores_of(qs[rows[u], :], ks[c : c + CHUNK, :])
                if causal and c < BLOCK:
                    s = jnp.where(ahead <= u * TILE - c, s, NEG)
                elif causal:
                    s = jnp.where(index >= (1 if c < 2 * BLOCK else 3), s, NEG)
                scores.append(s)
            every.append(scores)
        values = [functools.partial(take, vs, c, CHUNK) for c in range(0, 3 * BLOCK, CHUNK)]
        for u in range(UNROLL):
            keep(rows[u], one_pass(every[u], values, scale))

    if lead == 0:
        fast(0, True)

    def step(t, _):
        fast(t * BLOCK, False)
        return 0

    lax.fori_loop(1 if lead == 0 else 0, jnp.clip(sets - lead, 0, 2), step, 0)


def late_kernel(scale, first, at, *refs):
    if first == 0:
        q0, k2, v2, acc_a, ml_a, own_ref, lse_ref, vs, tail = refs
        jobs = [(0, q0, own_ref)]
    else:
        q1, q2, q3, k2, v2, acc_a, ml_a, acc_b, ml_b, p1, p2, p3, vs, tail = refs
        jobs = [(1, q1, p1), (2, q2, p2), (3, q3, p3)]
    index = at[0]
    sets = 4 - index // 4
    put_values(vs, 0, v2[...])
    row = lax.broadcasted_iota(jnp.int32, (LANES, LANES), 0)
    diagonal = row == lax.broadcasted_iota(jnp.int32, (LANES, LANES), 1)
    groups = TILE // LANES

    def finish(u, state, dest):
        top, total, acc = state
        dest[u * TILE : (u + 1) * TILE, :] = (acc / total).astype(dest.dtype)
        lse = top + jnp.log2(total)
        for g in range(groups):
            part = jnp.where(diagonal, lse[g * LANES : (g + 1) * LANES, :], 0.0)
            spot = u * groups + g
            tail[spot : spot + 1, :] = jnp.sum(part, axis=0, keepdims=True)

    def before(number):
        acc, ml = (acc_a, ml_a) if number < 4 else (acc_b, ml_b)
        rows = slice(number % 4 * TILE, (number % 4 + 1) * TILE)
        ml = ml[rows, :]
        return ml[:, 0:1], ml[:, LANES // 2 : LANES // 2 + 1], acc[rows, :]

    for n, query, dest in jobs:

        @pl.when((index >= 2) & (n < sets))
        def _():
            every = [
                [
                    scores_of(query[u * TILE : (u + 1) * TILE, :], k2[c : c + CHUNK, :])
                    for c in range(0, BLOCK, CHUNK)
                ]
                for u in range(UNROLL)
            ]
            values = [functools.partial(take, vs, c, CHUNK) for c in range(0, BLOCK, CHUNK)]
            for u in range(UNROLL):
                finish(u, one_pass(every[u], values, scale, before(n * UNROLL + u)), dest)

        @pl.when((index < 2) & (n < sets))
        def _():
            for u in range(UNROLL):
                top, total, acc = before(n * UNROLL + u)
                finish(u, (top, jnp.broadcast_to(total, acc.shape), acc), dest)

        @pl.when(n < sets)
        def _():
            if n == 0:
                lse_ref[...] = tail[...]
            else:
                value = tail[...]
                high = value.astype(jnp.bfloat16).astype(jnp.float32)
                middle = (value - high).astype(jnp.bfloat16).astype(jnp.float32)
                low = value - high - middle
                dest[BLOCK : BLOCK + TAIL, :] = jnp.concatenate(
                    [high, middle, low, jnp.zeros_like(low)], axis=0
                ).astype(jnp.bfloat16)

        @pl.when(n >= sets)
        def _():
            dest[...] = jnp.zeros_like(dest)


def near_kernel(scale, per_pos, positions, unroll, start, at, q, kv0, k1, v1, k2, v2, sinks, out_ref, ks, vs, fk, fv):
    index = at[0]
    ks[0:BLOCK, :] = k2[...]
    put_values(vs, 0, v2[...])
    ks[BLOCK : 2 * BLOCK, :] = k1[...]
    put_values(vs, BLOCK, v1[...])
    ks[2 * BLOCK : 3 * BLOCK, :] = kv0[0:BLOCK, :]
    put_values(vs, 2 * BLOCK, kv0[BLOCK : 2 * BLOCK, :])
    blank = jnp.zeros((LANES - SINK, LANES), jnp.bfloat16)
    fk[0:SINK, :] = sinks[0:SINK, :]
    fk[SINK:LANES, :] = blank
    put_values(fv, 0, sinks[SINK : 2 * SINK, :])
    put_values(fv, SINK, blank)
    tile = positions * per_pos
    width = WINDOW + positions
    row = lax.broadcasted_iota(jnp.int32, (tile, positions), 0) // per_pos
    col = lax.broadcasted_iota(jnp.int32, (tile, positions), 1)
    sink_row = lax.broadcasted_iota(jnp.int32, (tile, LANES), 0) // per_pos
    sink_col = lax.broadcasted_iota(jnp.int32, (tile, LANES), 1)
    first = (2 - index) * BLOCK
    cuts = [0, *range(positions, WINDOW, CHUNK), WINDOW, width]

    def group(t, partial_window):
        every, rows, begins = [], [], []
        for u in range(unroll):
            number = t * unroll + u
            rows.append(pl.ds(pl.multiple_of(number * tile, tile), tile))
            begin = pl.multiple_of(start + number * positions, positions)
            begins.append(begin)
            query = q[pl.ds(pl.multiple_of((start + number * positions) * per_pos, tile), tile), :]
            scores = []
            for low, high in zip(cuts, cuts[1:]):
                s = scores_of(query, ks[pl.ds(pl.multiple_of(begin + low, LANES), high - low), :])
                if partial_window:
                    column = lax.broadcasted_iota(jnp.int32, (1, high - low), 1) + begin + low
                    s = s + jnp.where(column >= first, 0.0, NEG)
                if low == 0:
                    s = jnp.where(col > row, s, NEG)
                if low == WINDOW:
                    s = jnp.where(col <= row, s, NEG)
                scores.append(s)
            far = scores_of(query, fk[...])
            reach = index * BLOCK + begin + sink_row - sink_col
            scores.append(jnp.where((sink_col < SINK) & (reach >= WINDOW), far, NEG))
            every.append(scores)
        for u in range(unroll):
            values = [
                functools.partial(take, vs, pl.multiple_of(begins[u] + low, LANES), high - low)
                for low, high in zip(cuts, cuts[1:])
            ]
            _, total, acc = one_pass(every[u], values + [functools.partial(take, fv, 0, LANES)], scale)
            out_ref[rows[u], :] = (acc / total).astype(out_ref.dtype)

    for cond, partial_window in ((index >= 2, False), (index < 2, True)):

        @pl.when(cond)
        def _():
            def step(t, _):
                group(t, partial_window)
                return 0

            lax.fori_loop(0, out_ref.shape[0] // (tile * unroll), step, 0)


def merge_kernel(norm, at, gate, own, lse, p1, p2, p3, near, grad, mix_ref, row_ref):
    level = at[0] // 4
    gated = gate[0]
    logs = [lse[...]]
    for n, ref in ((1, p1), (2, p2), (3, p3)):
        tail = ref[BLOCK : BLOCK + TAIL, :].astype(jnp.float32)
        value = tail[0:ROWS] + tail[ROWS : 2 * ROWS] + tail[2 * ROWS : 3 * ROWS]
        logs.append(jnp.where(level >= n, value, NEG))
    top = functools.reduce(jnp.maximum, logs)
    shares = [jnp.exp2(x - top) for x in logs]
    whole = functools.reduce(jnp.add, shares)
    shares = [x / whole for x in shares]
    total = jnp.zeros((1, LANES), jnp.float32)
    for g in range(BLOCK // LANES):
        rows = slice(g * LANES, (g + 1) * LANES)
        columns = [jnp.broadcast_to(x[g : g + 1, :], (LANES, LANES)).T for x in shares]
        full = columns[0] * own[rows, :]
        for column, ref in zip(columns[1:], (p1, p2, p3)):
            full = full + column * ref[rows, :].astype(jnp.float32)
        close = near[rows, :]
        mix_ref[rows, :] = (gated * full + (1.0 - gated) * close).astype(jnp.bfloat16)
        total = total + jnp.sum(
            grad[rows, :].astype(jnp.float32) * (full - close), axis=0, keepdims=True
        )
    value = jnp.sum(total, axis=1, keepdims=True) * norm
    lane = lax.broadcasted_iota(jnp.int32, row_ref.shape, 1)
    row_ref[...] = jnp.where(lane == at[1], value, 0.0)


def call(kernel, scalars, arrays, outs, scratch, estimate):
    specs = [pl.BlockSpec(memory_space=pltpu.SMEM)] * len(scalars)
    specs += [pl.BlockSpec(memory_space=VMEM)] * len(arrays)
    return pl.pallas_call(
        kernel,
        out_shape=outs,
        in_specs=specs,
        out_specs=[pl.BlockSpec(memory_space=VMEM)] * len(outs),
        scratch_shapes=scratch,
        compiler_params=params(),
        cost_estimate=estimate,
    )(*scalars, *arrays)


def shape(rows, dtype):
    return jax.ShapeDtypeStruct((rows, LANES), dtype)


def on_device(query_states, key_states, value_states, gate_values, head_flags, output_grad):
    bf16, f32 = jnp.bfloat16, jnp.float32
    heads = head_flags.shape[0]
    ctx = lax.axis_size("ctx")
    index = lax.axis_index("ctx")
    scale = LOG2E / math.sqrt(LANES)
    keys = key_states.reshape(BLOCK, LANES)
    values = value_states.reshape(BLOCK, LANES)
    marked = (head_flags == 1)[None, :, None]
    which = jnp.sum(head_flags * jnp.arange(heads, dtype=jnp.int32))

    at = jnp.stack([index, lax.axis_index("head") * heads + which, which]).astype(jnp.int32)

    def ring(block, shift):
        return lax.ppermute(block, "ctx", [(i, (i + shift) % ctx) for i in range(ctx)])

    def down(block, n):
        return lax.ppermute(block, "ctx", [(i, i - 4 * n) for i in range(4 * n, ctx)])

    def home(block, n):
        return lax.ppermute(block, "ctx", [(i - 4 * n, i) for i in range(4 * n, ctx)])

    trips = range(1, DEPTH + 1)
    kv0 = jnp.concatenate([keys, values], axis=0)
    k1, kv3 = ring(keys, 1), ring(kv0, 3)
    v1 = ring(lax.optimization_barrier((values, kv0))[0], 1)

    def sinks_of(first, second):
        return jnp.concatenate([first[:SINK], second[:SINK]], axis=0)

    flat = [a.reshape(BLOCK * heads, LANES) for a in (query_states, output_grad)]
    query, grad = pick(at, flat, heads)
    leaving, _ = lax.optimization_barrier((query, k1))
    visitors = [down(leaving, n) for n in trips]
    k2, v2 = ring(k1, 1), ring(kv3[BLOCK:], -1)
    gate = jnp.sum(jnp.where(head_flags == 1, gate_values, 0.0))[None]

    def early(lead, first, second):
        return call(
            functools.partial(early_kernel, scale, lead),
            [at],
            [first, second, kv0, k1, v1, kv3],
            [shape(2 * BLOCK, f32)] * 2,
            [
                VMEM((2 * BLOCK, LANES), bf16),
                VMEM((3 * BLOCK, LANES), bf16),
                VMEM((3 * BLOCK, 2 * LANES), bf16),
            ],
            cost(6),
        )

    early_states = early(0, query, visitors[0])
    early_states = [*early_states, *early(2, visitors[1], visitors[2])]
    sinks = sinks_of(keys, values)
    for place, pair in ((1, (k1, v1)), (2, (k2, v2)), (3, (kv3[:BLOCK], kv3[BLOCK:]))):
        sinks = jnp.where(index == place, sinks_of(*pair), sinks)
    level = index // 4
    moved = [
        lax.ppermute(sinks, "ctx", [(i, i + 4 * n) for i in range(4)]) for n in trips
    ]
    for n, got in zip(trips, moved):
        sinks = jnp.where(level == n, got, sinks)
    late_scratch = [VMEM((BLOCK, 2 * LANES), bf16), VMEM((ROWS, LANES), f32)]
    parts = call(
        functools.partial(late_kernel, scale, 1),
        [at],
        [*visitors, k2, v2, *early_states],
        [shape(BLOCK + TAIL, bf16)] * DEPTH,
        late_scratch,
        cost(3),
    )
    own_k2, _ = lax.optimization_barrier((k2, sinks))
    own, lse = call(
        functools.partial(late_kernel, scale, 0),
        [at],
        [query, own_k2, v2, *early_states[:2]],
        [shape(BLOCK, f32), shape(ROWS, f32)],
        late_scratch,
        cost(1),
    )
    parts = [home(part, n) for n, part in zip(trips, parts)]
    window = [kv0, k1, v1, k2, v2]
    scratch = [
        VMEM((3 * BLOCK, LANES), bf16),
        VMEM((3 * BLOCK, 2 * LANES), bf16),
        VMEM((LANES, LANES), bf16),
        VMEM((LANES, 2 * LANES), bf16),
    ]
    [near_one] = call(
        functools.partial(near_kernel, scale, 1, 256, 4, 0),
        [at],
        [query, *window, sinks],
        [shape(BLOCK, f32)],
        scratch,
        cost(2.5),
    )
    def near_part(start, count, sink_rows):
        return call(
            functools.partial(near_kernel, scale, heads, 128, 2, start),
            [at],
            [flat[0], *window, sink_rows],
            [shape(count * heads, bf16)],
            scratch,
            cost(9 * count / BLOCK),
        )[0]

    ahead = BLOCK // 4
    first_part = near_part(0, ahead, sinks)
    norm = 1.0 / math.sqrt(lax.axis_size("dp") * BLOCK * ctx * LANES)
    devices = lax.axis_size("dp") * lax.axis_size("head") * ctx
    mixed, row = call(
        functools.partial(merge_kernel, norm),
        [at, gate],
        [own, lse, *parts, near_one, grad],
        [shape(BLOCK, bf16), shape(devices, f32)],
        [],
        cost(0.1),
    )
    everyone = lax.all_to_all(row, ("dp", "head", "ctx"), 0, 0, tiled=True)
    gate_grad = jnp.sum(everyone, axis=0)[: heads * lax.axis_size("head")]
    later, _ = lax.optimization_barrier((sinks, row))
    near_all = jnp.concatenate([first_part, near_part(ahead, BLOCK - ahead, later)], axis=0)
    near_all = near_all.reshape(1, BLOCK, heads, LANES)
    blended = jnp.where(marked[None], mixed[None, :, None, :], near_all)
    return (blended, gate_grad)


def solution(mesh):
    spec = P("dp", "ctx", "head", None)
    return jax.shard_map(
        on_device,
        mesh=mesh,
        in_specs=(spec, spec, spec, P("head"), P("head"), spec),
        out_specs=(spec, P()),
        check_vma=False,
    )
```
